512 devices in a mesh: sess: 128 (over z, y, core), section: 4 (over x).
Axes of the slice: x: 4, y: 8, z: 8, core: 2. Of those that a mesh axis runs over, the one named last changes fastest.
Arguments:
- new_frames: bfloat16 [4, 1536, 16, 1536], P('section', 'sess'), may hold values from -6 to 6
- conv_edges: bfloat16 [4, 1536, 30, 1536], P('section', 'sess'), may hold values from -5 to 5
- kv_cache: bfloat16 [4, 1536, 64, 1536], P('section', 'sess'), may hold values from -240 to 240, as said below
- norm_gains: float32 [4, 2, 1536], P('section'), may hold values from 0.25 to 1.75
- conv_kernel: float32 [4, 31, 1536], P('section'), may hold values from -1 to 1
- w_qkv: bfloat16 [4, 1536, 2304], P('section', 'sess'), may hold values from -0.15625 to 0.15625
- w_out: bfloat16 [4, 768, 1536], P('section', 'sess'), may hold values from -0.21875 to 0.21875
- move_targets: int32 [1536], P('sess'), may hold values from 0 to 1535, as said below
- lengths: int32 [1536], P('sess'), may hold values from 0 to 64
- counts: int32 [128], P('sess'), may hold values from 6 to 12
Outputs:
- handed: bfloat16 [4, 1536, 16, 1536], P('section', 'sess')
The draws below stay inside these ranges and needn't reach their ends.
Inputs may be any that keep to these rules, and one draw needn't show every extreme that they name: `move_targets`: each index of sess hands exactly one live session to each of the indices 1 and 2 places away on either side, cyclically, and receives one from each; a session leaving for the index o places ahead is replaced by the one arriving from o places behind. All other sessions stay in their slots. `kv_cache`: values are of order one; keys may be up to 240 in magnitude.
All inputs are finite; a program needn't handle non-finite values.
Results may differ from the reference program's by a relative error of at most 0.0093.
The reference program's roundings to bfloat16 on the way (of `normed`, `projected`, `probs` and `context`) count: a program that leaves them out, or rounds other values in their place, can miss the bound.
Values may be sent and summed in bfloat16 or wider, within the bound.
A program may use at most 128 MiB of HBM per device.

```python
import jax
import jax.numpy as jnp
from jax import lax

D = 1536
HEADS = 8
HSIZE = 96
HD = 768
KERNEL = 31
EDGE = 30
CTX = 64
FR = 16
SLOTS = 12
SECTIONS = 4
SESSIONS = 1536
N_SESS = 128


def migration_plan(key):
    key_count, key_top, key_low, key_score = jax.random.split(key, 4)
    counts = jax.random.randint(key_count, (N_SESS,), SLOTS // 2, SLOTS + 1)
    highest = jax.random.randint(key_top, (), 0, N_SESS)
    lowest = (highest + 1 + jax.random.randint(key_low, (), 0, N_SESS - 1)) % N_SESS
    counts = counts.at[highest].set(SLOTS).at[lowest].set(SLOTS // 2)
    slot_ids = jnp.arange(SLOTS, dtype=jnp.int32)
    scores = jax.random.randint(key_score, (N_SESS, SLOTS), 0, 2 ** 20)
    scores = scores + jnp.where(slot_ids[None, :] >= counts[:, None], 2 ** 21, 0)
    order = jnp.argsort(scores, axis=1, stable=True).astype(jnp.int32)
    devices = jnp.arange(N_SESS, dtype=jnp.int32)
    targets = devices[:, None] * SLOTS + slot_ids[None, :]
    for round_index, offset in enumerate((1, -1, 2, -2)):
        receiver = (devices + offset) % N_SESS
        landing = receiver * SLOTS + order[receiver, round_index]
        targets = targets.at[devices, order[:, round_index]].set(landing)
    return (counts.astype(jnp.int32), targets.reshape(-1).astype(jnp.int32))


def draw_counts(key, part):
    counts, targets = migration_plan(key)
    return counts


def draw_move_targets(key, part):
    counts, targets = migration_plan(key)
    return targets


def draw_kv_cache(key, part):
    key = jax.random.fold_in(key, 11)
    key_main = jax.random.fold_in(key, 0)
    values = jnp.clip(jax.random.normal(key_main, (SECTIONS, SESSIONS, CTX, 2 * HD), jnp.float32), -4.0, 4.0)
    return values.astype(jnp.bfloat16)


def plant(entries, key, smallest, high):
    shape = entries.shape
    place = [jax.random.randint(jax.random.fold_in(key, axis), (), 0, shape[axis]) for axis in range(len(shape))]
    entries = entries.at[tuple(place)].set(smallest)
    longest = shape.index(max(shape))
    place[longest] = (place[longest] + 1) % shape[longest]
    return entries.at[tuple(place)].set(high)


def steps_of(stream_key, dims, shards, least, high):
    level, own = 1.0, jax.random.fold_in(stream_key, 6)
    for axis_at, shards_of in shards:
        draws = jnp.exp(jax.random.uniform(jax.random.fold_in(own, axis_at), (shards_of,), jnp.float32, least / len(shards), high / len(shards)))
        level = level * jnp.repeat(draws, dims[axis_at] // shards_of).reshape([-1 if axis == axis_at else 1 for axis in range(len(dims))])
    return level


def noise(rng, dims, scale, reach, cuts=(), held_as=jnp.bfloat16):
    values = jax.random.normal(rng, dims, jnp.float32) * scale
    if len(cuts) > 0:
        values = steps_of(rng, dims, cuts, -0.22, 0.18) * values
    return jnp.clip(values, min=-reach, max=reach).astype(held_as)


def setup_inputs(seed: int = 0) -> dict:
    arg_keys = jax.random.split(jax.random.key(seed), 11)
    return {
        "new_frames": noise(arg_keys[0], (SECTIONS, SESSIONS, FR, D), 1.0, 6.0, ((0, 4), (1, 128))),
        "conv_edges": noise(arg_keys[1], (SECTIONS, SESSIONS, EDGE, D), 1.0, 5.0, ((0, 4), (1, 128))),
        "kv_cache": draw_kv_cache(jax.random.fold_in(arg_keys[10], 71), 0),
        "norm_gains": jnp.clip(1.0 + 0.15 * jax.random.normal(arg_keys[3], (SECTIONS, 2, D), jnp.float32), 0.25, 1.75),
        "conv_kernel": noise(arg_keys[4], (SECTIONS, KERNEL, D), KERNEL ** -0.5, 1.0, ((0, 4),), jnp.float32),
        "w_qkv": noise(arg_keys[5], (SECTIONS, D, 3 * HD), D ** -0.5, 0.15625, ((0, 4), (1, 128))),
        "w_out": noise(arg_keys[6], (SECTIONS, HD, D), HD ** -0.5, 0.21875, ((0, 4), (1, 128))),
        "move_targets": draw_move_targets(jax.random.fold_in(arg_keys[10], 71), 0),
        "lengths": plant(jax.random.randint(arg_keys[8], (SESSIONS,), 0, CTX + 1), jax.random.fold_in(arg_keys[8], 1), 0, CTX).astype(jnp.int32),
        "counts": draw_counts(jax.random.fold_in(arg_keys[10], 71), 0),
    }


def layer_norm(values, gain):
    center = values - lax.optimization_barrier(jnp.mean(values, axis=-1, keepdims=True))
    spread = lax.optimization_barrier(jnp.mean(center * center, axis=-1, keepdims=True))
    return center * lax.rsqrt(spread + 1e-05) * gain

def attend(queries, keys, values, ctx_lengths):
    session_count = queries.shape[0]
    query_heads = queries.reshape(session_count, FR, HEADS, HSIZE).astype(jnp.float32)
    key_heads = keys.reshape(session_count, CTX + FR, HEADS, HSIZE).astype(jnp.float32)
    value_heads = values.reshape(session_count, CTX + FR, HEADS, HSIZE).astype(jnp.float32)
    scores = jnp.einsum('sthd,suhd->shtu', query_heads, key_heads) * HSIZE ** (-0.5)
    key_pos = jnp.arange(CTX + FR, dtype=jnp.int32)
    query_pos = jnp.arange(FR, dtype=jnp.int32)
    cached_ok = key_pos[None, :] >= (CTX - ctx_lengths)[:, None]
    fresh_ok = key_pos[None, :] - CTX <= query_pos[:, None]
    allowed = jnp.where(key_pos[None, None, :] < CTX, cached_ok[:, None, :], fresh_ok[None, :, :])
    scores = jnp.where(allowed[:, None, :, :], scores, jnp.float32(-1e+30))
    row_max = lax.optimization_barrier(jnp.max(scores, axis=-1, keepdims=True))
    weights = jnp.exp(scores - row_max)
    probs = (weights / lax.optimization_barrier(jnp.sum(weights, axis=-1, keepdims=True))).astype(jnp.bfloat16)
    context = jnp.einsum('shtu,suhd->sthd', probs.astype(jnp.float32), value_heads)
    return context.astype(jnp.bfloat16).reshape(session_count, FR, HD)

def section_block(frames, conv_edge, cache, ctx_lengths, norm_gains, kernel, wqkv, wout):
    session_count = frames.shape[0]
    normed = layer_norm(frames.astype(jnp.float32), norm_gains[0]).astype(jnp.bfloat16)
    sequence = jnp.concatenate([conv_edge, normed], axis=1).astype(jnp.float32)
    conv_out = jnp.zeros((session_count, FR, D), jnp.float32)
    for tap in range(KERNEL):
        conv_out = conv_out + kernel[tap] * sequence[:, tap:tap + FR]
    mid_state = frames.astype(jnp.float32) + conv_out
    second = layer_norm(mid_state, norm_gains[1]).astype(jnp.bfloat16)
    projected = jnp.dot(second.reshape(-1, D), wqkv, preferred_element_type=jnp.float32)
    projected = projected.astype(jnp.bfloat16).reshape(session_count, FR, 3 * HD)
    keys = jnp.concatenate([cache[:, :, :HD], projected[:, :, HD:2 * HD]], axis=1)
    values = jnp.concatenate([cache[:, :, HD:], projected[:, :, 2 * HD:]], axis=1)
    context = attend(projected[:, :, :HD], keys, values, ctx_lengths)
    output = jnp.dot(context.reshape(-1, HD), wout, preferred_element_type=jnp.float32)
    return mid_state + output.reshape(session_count, FR, D)

def reference(new_frames, conv_edges, kv_cache, norm_gains, conv_kernel, w_qkv, w_out, move_targets, lengths, counts):
    total = new_frames.shape[1]
    slot_ids = jnp.arange(total, dtype=jnp.int32)
    source = jnp.zeros((total,), jnp.int32).at[move_targets].set(slot_ids)
    live_mask = slot_ids % SLOTS < jnp.repeat(counts, SLOTS)
    results = []
    for section_index in range(SECTIONS):

        def one_block(block_index):
            first = (block_index * SLOTS).astype(jnp.int32)
            row_ids = first + jnp.arange(SLOTS, dtype=jnp.int32)
            source_slot = source[row_ids]
            frames = lax.dynamic_slice_in_dim(new_frames[section_index], first, SLOTS, 0)
            outcome = section_block(frames, conv_edges[section_index][source_slot], kv_cache[section_index][source_slot], lengths[row_ids], norm_gains[section_index], conv_kernel[section_index], w_qkv[section_index], w_out[section_index])
            keep = live_mask[row_ids][:, None, None]
            return jnp.where(keep, outcome, jnp.float32(0.0)).astype(jnp.bfloat16)
        blocks = lax.map(one_block, jnp.arange(N_SESS, dtype=jnp.int32))
        results.append(blocks.reshape(total, FR, D))
    return jnp.roll(jnp.stack(results), 1, axis=0)
```

```python
import functools

import jax
import jax.numpy as jnp
from jax import lax
from jax.experimental import pallas as pl
from jax.experimental.pallas import tpu as pltpu
from jax.sharding import PartitionSpec as P

D = 1536
HEADS = 8
HSIZE = 96
HD = 768
KERNEL = 31
EDGE = 30
CTX = 64
FR = 16
SLOTS = 12
RING = 8
N_SESS = 128
QW = 3 * HD
N0 = 1152
N1 = QW - N0
WIDTHS = (N0, N1)
STARTS = (0, N0)
OH = D // 2
OFFSETS = (1, -1, 2, -2)
MESH = pl.DeviceIdType.MESH
F32 = jnp.float32
BF16 = jnp.bfloat16


class Ring:
    def __init__(self, slot, me, plus, minus, send, recv, parts):
        self.slot, self.me, self.ids = slot, me, (plus, minus)
        self.send, self.recv, self.parts = send, recv, parts

    def hops(self, d, h):
        if self.parts == 1:
            return 4 - d
        return 4 if d == h else 3

    def group(self, d, k):
        return lax.rem(self.me + (RING - k if d == 0 else k), RING)

    def index(self, d, h, k):
        return (d * self.parts + h) * 4 + k - 1

    def copy(self, d, h, k, back):
        ref = self.slot(self.group(d, k - back), h)
        at = self.index(d, h, k)
        return pltpu.make_async_remote_copy(
            src_ref=ref,
            dst_ref=ref,
            send_sem=self.send.at[at],
            recv_sem=self.recv.at[at],
            device_id=self.ids[d],
            device_id_type=MESH,
        )

    def start(self):
        for h in range(self.parts):
            for d in ((0, 1) if h == 0 else (1, 0)):
                self.copy(d, h, 1, 1).start()

    def arrive(self, d, h, k):
        if k > self.hops(d, h):
            return False
        self.copy(d, h, k, 0).wait_recv()
        if k < self.hops(d, h):
            self.copy(d, h, k + 1, 1).start()
        return True

    def drain(self):
        for h in range(self.parts):
            for d in range(2):
                for k in range(1, self.hops(d, h) + 1):
                    self.copy(d, h, k, 1).wait_send()


def share_index(d, h, k):
    return h if k == 0 else 2 + (d * 2 + h) * 4 + k - 1


def every_share():
    out = [(0, 0, 0), (0, 1, 0)]
    for d in range(2):
        for h in range(2):
            for k in range(1, (4 if d == h else 3) + 1):
                out.append((d, h, k))
    return out


def layer_norm(values, gain):
    center = values - jnp.mean(values, axis=-1, keepdims=True)
    spread = jnp.mean(center * center, axis=-1, keepdims=True)
    return center * lax.rsqrt(spread + 1e-05) * gain


def kernel(
    frames, edges, cache, gains, taps, wq, wo, targets, lengths, counts,
    out,
    e_loc, c_loc, e_stage, c_stage, e_arr, c_arr,
    x_q0, x_q1, x_o, bufq0, bufq1, p1o, bufo,
    tmp_q, tmp_o, seq, mid, second, proj, ctx, hmask, ostage,
    loc_sem, x_send, x_recv, m_send, m_recv,
    pq_send, pq_recv, po_send, po_recv,
    qq_send, qq_recv, qo_send, qo_recv,
    sq_send, sq_recv, so_send, so_recv,
    h_send, h_recv,
):
    sess = lax.axis_index("sess")
    sec = lax.axis_index("section")
    nsec = lax.axis_size("section")
    core = lax.rem(sess, 2)
    chip = sess // 2
    y = lax.rem(chip, RING)
    z = chip // RING

    def at(zz, yy, cc):
        return ((zz * RING + yy) * 2 + cc, sec)

    def step(v, by):
        return lax.rem(v + RING + by, RING)

    sib = at(z, y, 1 - core)
    y_ids = (at(z, step(y, 1), core), at(z, step(y, -1), core))
    z_ids = (at(step(z, 1), y, core), at(step(z, -1), y, core))
    next_sec = (sess, lax.rem(sec + 1, nsec))
    prev_sec = (sess, lax.rem(sec + nsec - 1, nsec))
    moves = [(lax.rem(sess + N_SESS + o, N_SESS), sec) for o in OFFSETS]
    bufq = (bufq0, bufq1)
    x_q = (x_q0, x_q1)

    def by_role(fn):
        for role in range(2):
            @pl.when(core == role)
            def _():
                fn(role)

    load_e = pltpu.make_async_copy(edges, e_loc, loc_sem.at[0])
    load_c = pltpu.make_async_copy(cache, c_loc, loc_sem.at[1])
    load_e.start()
    load_c.start()

    barrier = pltpu.get_barrier_semaphore()
    greet = [*moves, *y_ids, *z_ids, sib, next_sec, prev_sec]
    for dev in greet:
        pl.semaphore_signal(barrier, inc=1, device_id=dev, device_id_type=MESH)

    wanted = [m[0] * SLOTS for m in moves]

    def hits(j):
        t = targets[j]
        return [(t >= w) & (t < w + SLOTS) for w in wanted]

    picks = [jnp.int32(0)] * 4
    for j in range(SLOTS):
        picks = [jnp.where(hit, jnp.int32(j), p) for hit, p in zip(hits(j), picks)]

    def source(j):
        found = hits(j)
        arrived = found[0] | found[1] | found[2] | found[3]
        place = jnp.int32(0)
        for r in range(1, 4):
            place = jnp.where(found[r], jnp.int32(r), place)
        return arrived, place

    def pick(arrived, there, here):
        return jnp.where(arrived, there, here)

    pl.semaphore_wait(barrier, len(greet))

    def swap_q(role, dst_role):
        return pltpu.make_async_remote_copy(
            src_ref=wq.at[:, pl.ds(STARTS[dst_role], WIDTHS[dst_role])],
            dst_ref=x_q[dst_role],
            send_sem=x_send.at[0],
            recv_sem=x_recv.at[0],
            device_id=sib,
            device_id_type=MESH,
        )

    def swap_o(role):
        return pltpu.make_async_remote_copy(
            src_ref=wo.at[:, pl.ds((1 - role) * OH, OH)],
            dst_ref=x_o,
            send_sem=x_send.at[1],
            recv_sem=x_recv.at[1],
            device_id=sib,
            device_id_type=MESH,
        )

    def start_swap(role):
        swap_q(role, 1 - role).start()
        swap_o(role).start()

    by_role(start_swap)

    def migrate(r, stage, arr, base):
        return pltpu.make_async_remote_copy(
            src_ref=stage.at[r],
            dst_ref=arr.at[r],
            send_sem=m_send.at[base + r],
            recv_sem=m_recv.at[base + r],
            device_id=moves[r],
            device_id_type=MESH,
        )

    load_e.wait()
    for r in range(4):
        e_stage[r] = e_loc[picks[r]]
        migrate(r, e_stage, e_arr, 0).start()

    def q_slot_block(role):
        if role == 0:
            return lambda g, h: bufq0.at[z, g]
        return lambda g, h: bufq1.at[g, y]

    def q_slot_group(role):
        if role == 0:
            return lambda g, h: bufq0.at[g, pl.ds(4 * h, 4)]
        return lambda g, h: bufq1.at[pl.ds(4 * h, 4), g]

    def ring_pq(role):
        me, ids = ((y, y_ids), (z, z_ids))[role]
        return Ring(q_slot_block(role), me, *ids, pq_send, pq_recv, 1)

    def ring_qq(role):
        me, ids = ((z, z_ids), (y, y_ids))[role]
        return Ring(q_slot_group(role), me, *ids, qq_send, qq_recv, 2)

    ring_po = Ring(lambda g, h: p1o.at[g], y, *y_ids, po_send, po_recv, 1)
    ring_qo = Ring(
        lambda g, h: bufo.at[core, g, pl.ds(48 * h, 48)], z, *z_ids, qo_send, qo_recv, 2
    )

    def enter_q(role):
        n = WIDTHS[role]
        swap_q(role, role).wait_recv()
        own = wq[:, STARTS[role]:STARTS[role] + n].astype(F32)
        other = x_q[role][...].astype(F32)
        if role == 0:
            tmp_q[0:12, 0:n] = own
            tmp_q[12:24, 0:n] = other
        else:
            tmp_q[0:12, 0:n] = other
            tmp_q[12:24, 0:n] = own
        bufq[role][z, y] = tmp_q[:, 0:n].astype(BF16)
        ring_pq(role).start()

    by_role(enter_q)

    def enter_o(role):
        swap_o(role).wait_recv()
        own = wo[:, role * OH:(role + 1) * OH].astype(F32)
        other = x_o[...].astype(F32)
        first, last = (own, other) if role == 0 else (other, own)
        tmp_o[0:6, :] = first
        tmp_o[6:12, :] = last

    by_role(enter_o)
    p1o[y] = tmp_o[0:12, :].astype(BF16)
    ring_po.start()

    head_of_row = lax.broadcasted_iota(jnp.int32, (HEADS * FR, HD), 0) // FR
    lane = lax.broadcasted_iota(jnp.int32, (HEADS * FR, HD), 1)
    inside = (lane >= head_of_row * HSIZE) & (lane < head_of_row * HSIZE + HSIZE)
    hmask[...] = jnp.where(inside, 1.0, 0.0).astype(BF16)
    load_c.wait()
    for r in range(4):
        c_stage[r] = c_loc[picks[r]]

    for k in range(1, 5):
        def go(role):
            ring = ring_pq(role)
            ring.arrive(0, 0, k)
            ring.arrive(1, 0, k)
        by_role(go)
        ring_po.arrive(0, 0, k)
        ring_po.arrive(1, 0, k)

    def share(role, d, h, k, q):
        if q:
            ring = ring_qq(role)
            sems = (sq_send, sq_recv)
        else:
            ring = ring_qo
            sems = (so_send, so_recv)
        ref = ring.slot(ring.group(d, k), h)
        i = share_index(d, h, k)
        return pltpu.make_async_remote_copy(
            src_ref=ref,
            dst_ref=ref,
            send_sem=sems[0].at[i],
            recv_sem=sems[1].at[i],
            device_id=sib,
            device_id_type=MESH,
        )

    def start_qq(role):
        ring_qq(role).start()
        share(role, 0, 0, 0, True).start()
        share(role, 0, 1, 0, True).start()

    by_role(start_qq)
    for r in range(4):
        migrate(r, c_stage, c_arr, 4).start()

    for p in range(RING):
        tmp_o[12 * p:12 * p + 12, :] = p1o[p].astype(F32)
    bufo[core, z] = tmp_o[...].astype(BF16)

    def start_qo():
        ring_qo.start()
        share(0, 0, 0, 0, False).start()
        share(0, 0, 1, 0, False).start()

    def serve_q(h, k):
        def go(role):
            ring = ring_qq(role)
            for d in ((0, 1) if h == 0 else (1, 0)):
                if ring.arrive(d, h, k):
                    share(role, d, h, k, True).start()
        by_role(go)

    def serve_o(k):
        for h in range(2):
            for d in range(2):
                if ring_qo.arrive(d, h, k):
                    share(0, d, h, k, False).start()

    for r in range(4):
        migrate(r, e_stage, e_arr, 0).wait_recv()

    def front(j, carry):
        x = frames[j].astype(F32)
        normed = layer_norm(x, gains[0:1, :]).astype(BF16)
        arrived, place = source(j)
        seq[0:EDGE, :] = pick(arrived, e_arr[place], e_loc[j]).astype(F32)
        seq[EDGE:EDGE + FR, :] = normed.astype(F32)
        rows = pl.ds(pl.multiple_of(j * FR, FR), FR)
        for c in range(D // 128):
            lanes = slice(128 * c, 128 * c + 128)
            total = taps[0:1, lanes] * seq[0:FR, lanes]
            for t in range(1, KERNEL):
                total = total + taps[t:t + 1, lanes] * seq[t:t + FR, lanes]
            mid[rows, lanes] = frames[j, :, lanes].astype(F32) + total
        second[rows, :] = layer_norm(mid[rows, :], gains[1:2, :]).astype(BF16)
        return carry

    for k in range(1, 4):
        for h in range(2):
            i = 2 * ((k - 1) * 2 + h)
            lax.fori_loop(i, i + 2, front, 0)
            serve_q(h, k)
    start_qo()
    serve_q(0, 4)
    serve_q(1, 4)

    def shared_q(role):
        for d, h, k in every_share():
            share(1 - role, d, h, k, True).wait_recv()

    by_role(shared_q)

    for role in range(2):
        n = WIDTHS[role]
        total = jnp.zeros((SLOTS * FR, n), F32)
        for g in range(4):
            part = bufq[role][2 * g:2 * g + 2].astype(F32).reshape(384, n).astype(BF16)
            total = total + jnp.dot(
                second[:, 384 * g:384 * g + 384], part, preferred_element_type=F32
            )
        proj[:, STARTS[role]:STARTS[role] + n] = total.astype(BF16)
        serve_o(1 + role)

    for r in range(4):
        migrate(r, c_stage, c_arr, 4).wait_recv()

    key_pos = lax.broadcasted_iota(jnp.int32, (HEADS * FR, CTX + FR), 1)
    frame = lax.rem(lax.broadcasted_iota(jnp.int32, (HEADS * FR, CTX + FR), 0), FR)

    def attend(j, carry):
        rows = pl.ds(pl.multiple_of(j * FR, FR), FR)
        arrived, place = source(j)
        cached = pick(arrived, c_arr[place], c_loc[j])
        keys = jnp.concatenate([cached[:, :HD], proj[rows, HD:2 * HD]], axis=0)
        values = jnp.concatenate([cached[:, HD:], proj[rows, 2 * HD:]], axis=0)
        q = proj[rows, :HD]
        queries = jnp.concatenate([q] * HEADS, axis=0) * hmask[...]
        scores = lax.dot_general(
            queries, keys, (((1,), (1,)), ((), ())), preferred_element_type=F32
        ) * HSIZE ** (-0.5)
        allowed = ((key_pos < CTX) & (key_pos >= CTX - lengths[j])) | (
            (key_pos >= CTX) & (key_pos - CTX <= frame)
        )
        scores = jnp.where(allowed, scores, -1e30)
        weights = jnp.exp(scores - jnp.max(scores, axis=-1, keepdims=True))
        probs = (weights / jnp.sum(weights, axis=-1, keepdims=True)).astype(BF16)
        wide = jnp.dot(probs, values, preferred_element_type=F32)
        wide = wide * hmask[...].astype(F32)
        total = wide[0:FR]
        for hd in range(1, HEADS):
            total = total + wide[FR * hd:FR * hd + FR]
        ctx[rows, :] = total.astype(BF16)
        return carry

    lax.fori_loop(0, 6, attend, 0)
    serve_o(3)
    lax.fori_loop(6, SLOTS, attend, 0)
    serve_o(4)

    def shared_o(role):
        for d, h, k in every_share():
            i = share_index(d, h, k)
            ref = bufo.at[1 - core, ring_qo.group(d, k), pl.ds(48 * h, 48)]
            pltpu.make_async_remote_copy(
                src_ref=ref,
                dst_ref=ref,
                send_sem=so_send.at[i],
                recv_sem=so_recv.at[i],
                device_id=sib,
                device_id_type=MESH,
            ).wait_recv()

    shared_o(0)

    def hand(n):
        lanes = pl.ds(384 * n, 384)
        return pltpu.make_async_remote_copy(
            src_ref=ostage.at[:, :, lanes],
            dst_ref=out.at[:, :, lanes],
            send_sem=h_send.at[n],
            recv_sem=h_recv.at[n],
            device_id=next_sec,
            device_id_type=MESH,
        )

    for n in range(4):
        lanes = slice(384 * n, 384 * n + 384)
        half, at_lane = n // 2, 384 * (n % 2)
        weights = bufo[half, :, :, at_lane:at_lane + 384].reshape(HD, 384)
        result = jnp.dot(ctx[...], weights, preferred_element_type=F32) + mid[:, lanes]
        for j in range(SLOTS):
            live = counts[0] > j
            ostage[j, :, lanes] = jnp.where(
                live, result[FR * j:FR * j + FR], 0.0
            ).astype(BF16)
        hand(n).start()

    def drain_role(role):
        swap_q(role, 1 - role).wait_send()
        swap_o(role).wait_send()
        ring_pq(role).drain()
        ring_qq(role).drain()
        for d, h, k in every_share():
            share(role, d, h, k, True).wait_send()

    by_role(drain_role)
    ring_po.drain()
    ring_qo.drain()
    for d, h, k in every_share():
        share(0, d, h, k, False).wait_send()
    for r in range(4):
        migrate(r, e_stage, e_arr, 0).wait_send()
        migrate(r, c_stage, c_arr, 4).wait_send()
    for n in range(4):
        hand(n).wait_send()
        hand(n).wait_recv()


def body(
    new_frames, conv_edges, kv_cache, norm_gains, conv_kernel,
    w_qkv, w_out, move_targets, lengths, counts,
):
    vmem = pl.BlockSpec(memory_space=pltpu.VMEM)
    smem = pl.BlockSpec(memory_space=pltpu.SMEM)
    any_ = pl.BlockSpec(memory_space=pl.ANY)
    dma = pltpu.SemaphoreType.DMA
    rows = SLOTS * FR
    out = pl.pallas_call(
        kernel,
        out_shape=jax.ShapeDtypeStruct((SLOTS, FR, D), BF16),
        in_specs=[vmem, any_, any_, vmem, vmem, vmem, vmem, smem, smem, smem],
        out_specs=any_,
        scratch_shapes=[
            pltpu.VMEM((SLOTS, EDGE, D), BF16),
            pltpu.VMEM((SLOTS, CTX, D), BF16),
            pltpu.VMEM((4, EDGE, D), BF16),
            pltpu.VMEM((4, CTX, D), BF16),
            pltpu.VMEM((4, EDGE, D), BF16),
            pltpu.VMEM((4, CTX, D), BF16),
            pltpu.VMEM((12, N0), BF16),
            pltpu.VMEM((12, N1), BF16),
            pltpu.VMEM((6, OH), BF16),
            pltpu.VMEM((RING, RING, 24, N0), BF16),
            pltpu.VMEM((RING, RING, 24, N1), BF16),
            pltpu.VMEM((RING, 12, OH), BF16),
            pltpu.VMEM((2, RING, 96, OH), BF16),
            pltpu.VMEM((24, max(N0, N1)), F32),
            pltpu.VMEM((96, OH), F32),
            pltpu.VMEM((48, D), F32),
            pltpu.VMEM((rows, D), F32),
            pltpu.VMEM((rows, D), BF16),
            pltpu.VMEM((rows, QW), BF16),
            pltpu.VMEM((rows, HD), BF16),
            pltpu.VMEM((HEADS * FR, HD), BF16),
            pltpu.VMEM((SLOTS, FR, D), BF16),
            dma((2,)), dma((2,)), dma((2,)), dma((8,)), dma((8,)),
            dma((8,)), dma((8,)), dma((8,)), dma((8,)),
            dma((16,)), dma((16,)), dma((16,)), dma((16,)),
            dma((18,)), dma((18,)), dma((18,)), dma((18,)),
            dma((4,)), dma((4,)),
        ],
        compiler_params=pltpu.CompilerParams(
            collective_id=0, has_side_effects=True, vmem_limit_bytes=56 * 2 ** 20
        ),
        cost_estimate=pl.CostEstimate(
            flops=2 * 10 ** 9, bytes_accessed=6 * 10 ** 6, transcendentals=10 ** 5
        ),
    )(
        new_frames[0], conv_edges[0], kv_cache[0], norm_gains[0], conv_kernel[0],
        w_qkv[0], w_out[0], move_targets, lengths, counts,
    )
    return out[None]


def solution(mesh):
    placed = (
        P("section", "sess", None, None),
        P("section", "sess", None, None),
        P("section", "sess", None, None),
        P("section", None, None),
        P("section", None, None),
        P("section", "sess", None),
        P("section", "sess", None),
        P("sess"),
        P("sess"),
        P("sess"),
    )
    return jax.shard_map(
        body,
        mesh=mesh,
        in_specs=placed,
        out_specs=P("section", "sess", None, None),
        check_vma=False,
    )
```

```python
import functools

import jax
import jax.numpy as jnp
from jax import lax
from jax.experimental import pallas as pl
from jax.experimental.pallas import tpu as pltpu
from jax.sharding import PartitionSpec as P

D = 1536
HEADS = 8
HSIZE = 96
HD = 768
KERNEL = 31
EDGE = 30
CTX = 64
FR = 16
SLOTS = 12
RING = 8
N_SESS = 128
QW = 3 * HD
OH = D // 2
WIDTHS = (2 * HD, HD)
STARTS = (0, 2 * HD)
PART = HD // 2
GROUP = 4
LAST = RING - 1
TILES = ((0, 3), (2, 6), (5, 8))
TILE_ROWS = ((0, 48), (48, 112), (112, 160))
OFFSETS = (1, -1, 2, -2)
MESH = pl.DeviceIdType.MESH
F32 = jnp.float32
BF16 = jnp.bfloat16


class Book:
    def __init__(self):
        self.started, self.arrived, self.left = {}, set(), set()

    def start(self, role, make, key):
        make().start()
        self.started[(role, key)] = make

    def arrive(self, role, make, key):
        make().wait_recv()
        self.arrived.add((role, key))

    def sent(self, role, key):
        self.started[(role, key)]().wait_send()
        self.left.add((role, key))

    def close(self, role):
        for key, make in self.started.items():
            if key[0] == role and key not in self.left:
                make().wait_send()
            if key[0] == role and key not in self.arrived:
                make().wait_recv()


def hops(d, h):
    return 4 if d == h else 3


def turn(me, by):
    return lax.rem(me + (by % RING), RING)


def every_share():
    out = [(0, 0, 0), (0, 1, 0)]
    for d in range(2):
        for h in range(2):
            for k in range(1, hops(d, h) + 1):
                out.append((d, h, k))
    return out


def remote(src, dst, send, recv, i, dev):
    return pltpu.make_async_remote_copy(
        src_ref=src,
        dst_ref=dst,
        send_sem=send.at[i],
        recv_sem=recv.at[i],
        device_id=dev,
        device_id_type=MESH,
    )


class Spread:
    def __init__(self, book, role, name, slot, me, ids, sems):
        self.book, self.role, self.name = book, role, name
        self.slot, self.me, self.ids, self.sems = slot, me, ids, sems

    def copy(self, d, h, back):
        ref = self.slot(turn(self.me, back), h)
        return remote(ref, ref, *self.sems, 8 * h + d - 1, self.ids(d))

    def start(self, h):
        for d in (1, 7, 2, 6, 3, 5, 4):
            make = lambda d=d: self.copy(d, h, 0)
            self.book.start(self.role, make, (self.name, d, h))

    def arrive(self, h):
        for d in (1, 7, 2, 6, 3, 5, 4):
            self.book.arrive(self.role, lambda: self.copy(d, h, -d), (self.name, d, h))


class Ring:
    def __init__(self, book, role, name, slot, me, place, away, sib, sems, share_sems):
        self.book, self.role, self.name = book, role, name
        self.slot, self.me, self.place, self.away = slot, me, place, away
        self.sib, self.sems, self.share_sems = sib, sems, share_sems

    def group(self, d, k):
        return turn(self.me, -k if d == 0 else k)

    def copy(self, d, h, k, back):
        ref = self.slot(self.group(d, k - back), h)
        to = self.place(turn(self.me, 1 - 2 * d))
        return remote(ref, ref, *self.sems, (d * 2 + h) * 4 + k - 1, to)

    def last(self, h, back):
        away = self.away[h]
        group = lax.rem(self.me + 5 + 6 * away, RING) if back else turn(self.me, 4)
        ref = self.slot(group, h)
        to = self.place(lax.rem(self.me + 1 + 6 * away, RING))
        return remote(ref, ref, *self.sems, 12 * h + 3, to)

    def share(self, d, h, k):
        ref = self.slot(self.group(d, k), h)
        i = h if k == 0 else 2 + (d * 2 + h) * 4 + k - 1
        return remote(ref, ref, *self.share_sems, i, self.sib)

    def pass_on(self, d, h, k):
        make = lambda: self.copy(d, h, k + 1, 1)
        self.book.start(self.role, make, (self.name, d, h, k + 1))

    def give(self, d, h, k):
        self.book.start(self.role, lambda: self.share(d, h, k), (self.name, "s", d, h, k))

    def start(self, h):
        for d in (h, 1 - h):
            self.pass_on(d, h, 0)
        self.give(0, h, 0)

    def serve(self, h, k):
        if k == 4:
            self.book.arrive(self.role, lambda: self.last(h, 0), (self.name, h, h, 4))
            self.give(h, h, 4)
            return
        for d in (h, 1 - h):
            self.book.arrive(self.role, lambda: self.copy(d, h, k, 0), (self.name, d, h, k))
            if k < 3:
                self.pass_on(d, h, k)
                self.give(d, h, k)
        if k == 3:
            make = lambda: self.last(h, 1)
            self.book.start(self.role, make, (self.name, h, h, 4))
            for d in (h, 1 - h):
                self.give(d, h, k)

    def shared(self, book_role, parts=(0, 1)):
        for d, h, k in every_share():
            if h in parts:
                self.book.arrive(book_role, lambda: self.share(d, h, k), (self.name, "s", d, h, k))


def layer_norm(values, gain):
    center = values - jnp.mean(values, axis=-1, keepdims=True)
    spread = jnp.mean(center * center, axis=-1, keepdims=True)
    return center * lax.rsqrt(spread + 1e-05) * gain


def kernel(
    frames_in, edges, cache, gains, taps_in, wq_in, wo_in, targets, lengths, counts,
    out,
    frames, taps, wq, wo,
    e_loc, c_loc, e_stage, c_stage, e_arr, c_arr, e_via, c_via,
    x_q0, x_q1, x_o, bufq0, bufq1, p1o, bufo,
    tmp_q, tmp_o, seq, mid, second, proj, ctx, hmask, fmask, order, ostage,
    loc_sem, x_send, x_recv, m_send, m_recv,
    pq_send, pq_recv, po_send, po_recv,
    qq_send, qq_recv, qo_send, qo_recv,
    sq_send, sq_recv, so_send, so_recv,
    h_send, h_recv, v_send, v_recv,
):
    sess = lax.axis_index("sess")
    sec = lax.axis_index("section")
    nsec = lax.axis_size("section")
    core = lax.rem(sess, 2)
    y = lax.rem(sess // 2, RING)
    z = sess // (2 * RING)
    book = Book()

    def at(zz, yy, cc):
        return ((zz * RING + yy) * 2 + cc, sec)

    def on_y(d):
        return at(z, turn(y, d), core)

    def on_z(d):
        return at(turn(z, d), y, core)

    sib = at(z, y, 1 - core)
    next_sec = (sess, lax.rem(sec + 1, nsec))
    prev_sec = (sess, lax.rem(sec + nsec - 1, nsec))
    moves = [(lax.rem(sess + N_SESS + o, N_SESS), sec) for o in OFFSETS]
    bufq = (bufq0, bufq1)
    x_q = (x_q0, x_q1)

    def by_role(fn):
        for role in range(2):
            @pl.when(core == role)
            def _():
                fn(role)

    barrier = pltpu.get_barrier_semaphore()
    greet = [*moves, sib, next_sec, prev_sec, at(z, LAST - y, 1 - core)]
    greet += [on_y(d) for d in range(1, RING)] + [on_z(d) for d in range(1, RING)]
    for dev in greet:
        pl.semaphore_signal(barrier, inc=1, device_id=dev, device_id_type=MESH)

    loads = [
        pltpu.make_async_copy(src, dst, loc_sem.at[i])
        for i, (src, dst) in enumerate(
            ((wq_in, wq), (wo_in, wo), (edges, e_loc), (cache, c_loc),
             (frames_in, frames), (taps_in, taps))
        )
    ]
    for load in loads:
        load.start()

    wanted = [m[0] * SLOTS for m in moves]

    def hits(j):
        t = targets[j]
        return [(t >= w) & (t < w + SLOTS) for w in wanted]

    picks = [jnp.int32(0)] * 4
    for j in range(SLOTS):
        picks = [jnp.where(hit, jnp.int32(j), p) for hit, p in zip(hits(j), picks)]

    def source(j):
        found = hits(j)
        arrived = found[0] | found[1] | found[2] | found[3]
        place = jnp.int32(0)
        for r in range(1, 4):
            place = jnp.where(found[r], jnp.int32(r), place)
        return arrived, place

    for load in loads[:3]:
        load.wait()
    pl.semaphore_wait(barrier, len(greet))

    def swap_q(dst_role):
        return remote(
            wq.at[:, pl.ds(STARTS[dst_role], WIDTHS[dst_role])],
            x_q[dst_role], x_send, x_recv, 0, sib,
        )

    def swap_o(role):
        return remote(wo.at[:, pl.ds((1 - role) * OH, OH)], x_o, x_send, x_recv, 1, sib)

    def start_swap(role):
        book.start(role, lambda: swap_q(1 - role), "xq")
        book.start(role, lambda: swap_o(role), "xo")

    by_role(start_swap)

    def copy_e(r):
        return remote(e_stage.at[r], e_arr.at[r], m_send, m_recv, r, moves[r])

    def copy_c(r):
        return remote(c_stage.at[r], c_arr.at[r], m_send, m_recv, 4 + r, moves[r])

    crossing = [(y == LAST) & (core == 1), (y == 0) & (core == 0), y == LAST, y == 0]
    parts = ((e_stage, e_via, e_arr), (c_stage, c_via, c_arr))

    def across_z(m, r):
        stage, via, _ = parts[m]
        i = 2 * m + r // 2
        return remote(
            stage.at[r], via.at[r // 2], v_send, v_recv, i, on_z(1 if r % 2 == 0 else -1)
        )

    def along_y(m, r):
        _, via, arr = parts[m]
        to = at(z, LAST - y, core if r >= 2 else 1 - core)
        return remote(via.at[r // 2], arr.at[r], m_send, m_recv, 4 * m + r, to)

    def leave_row(m):
        for r in range(4):
            @pl.when(crossing[r])
            def _():
                book.start(("z", r), lambda r=r: across_z(m, r), ("z", m))

    def leave(m):
        for r in range(4):
            @pl.when(jnp.logical_not(crossing[r]))
            def _():
                book.start(("d", r), lambda r=r: (copy_e, copy_c)[m](r), ("d", m))
                book.arrived.add((("d", r), ("d", m)))

    def pass_along(m):
        for r in range(4):
            @pl.when(crossing[r])
            def _():
                book.arrive(("z", r), lambda r=r: across_z(m, r), ("z", m))
                book.start(("z", r), lambda r=r: along_y(m, r), ("y", m))
                book.arrived.add((("z", r), ("y", m)))

    for r in range(4):
        e_stage[r] = e_loc[picks[r]]
    leave_row(0)
    loads[3].wait()
    for r in range(4):
        c_stage[r] = c_loc[picks[r]]
    leave_row(1)

    def q_block(role):
        if role == 0:
            return lambda g, h: bufq0.at[h, z, g]
        return lambda g, h: bufq1.at[h, g, y]

    def q_group(role):
        if role == 0:
            return lambda g, h: bufq0.at[h, g]
        return lambda g, h: bufq1.at[h, :, g]

    along, across = (y, z), (z, y)
    on_along = (on_y, on_z)
    across_at = (lambda v: at(v, y, core), lambda v: at(z, v, core))
    away = ((0, 1), (0, 1))
    spread_q = [
        Spread(book, role, "pq", q_block(role), along[role], on_along[role],
               (pq_send, pq_recv))
        for role in range(2)
    ]
    ring_q = [
        Ring(book, role, "qq", q_group(role), across[role], across_at[role], away[role], sib,
             (qq_send, qq_recv), (sq_send, sq_recv))
        for role in range(2)
    ]
    spread_o = [
        Spread(book, role, "po", lambda g, h: p1o.at[g], along[role], on_along[role],
               (po_send, po_recv))
        for role in range(2)
    ]
    ring_o = [
        Ring(book, role, "qo", lambda g, h, role=role: bufo.at[role, h, g], across[role],
             across_at[role], away[role], sib, (qo_send, qo_recv), (so_send, so_recv))
        for role in range(2)
    ]

    def joined(role, n, own, other):
        first, last = (own, other) if role == 0 else (other, own)
        return first.astype(F32), last.astype(F32)

    def enter_q(role):
        book.arrive(role, lambda: swap_q(role), "xq")
        width = WIDTHS[role] // 2
        for h in range(2):
            for m in range(0, width, PART):
                lanes = slice(2 * m + PART * h, 2 * m + PART * h + PART)
                own = wq[:, STARTS[role] + lanes.start:STARTS[role] + lanes.stop]
                first, last = joined(role, 12, own, x_q[role][:, lanes])
                tmp_q[0:12, m:m + PART] = first
                tmp_q[12:24, m:m + PART] = last
            bufq[role][h, z, y] = tmp_q[:, 0:width].astype(BF16)
            spread_q[role].start(h)

    by_role(enter_q)
    leave(0)

    def enter_o(role):
        book.arrive(role, lambda: swap_o(role), "xo")
        first, last = joined(role, 6, wo[:, role * OH:(role + 1) * OH], x_o[...])
        tmp_o[0:6, :] = first
        tmp_o[6:12, :] = last
        p1o[along[role]] = tmp_o[0:12, :].astype(BF16)

    by_role(enter_o)

    for (low, high), (top, end) in zip(TILES, TILE_ROWS):
        shape = (end - top, 256)
        head = lax.broadcasted_iota(jnp.int32, shape, 0) // FR + low
        lane = lax.broadcasted_iota(jnp.int32, shape, 1) + 256 * TILES.index((low, high))
        inside = (lane >= head * HSIZE) & (lane < head * HSIZE + HSIZE)
        fmask[top:end, :] = jnp.where(inside, 1.0, 0.0)
        hmask[top:end, :] = jnp.where(inside, 1.0, 0.0).astype(BF16)
    for load in loads[4:]:
        load.wait()

    def start_q(role):
        for h in range(2):
            spread_q[role].arrive(h)
            ring_q[role].start(h)
        spread_o[role].start(0)

    by_role(start_q)
    pass_along(0)
    leave(1)
    pass_along(1)

    for i in range(HD // 128):
        shape = (HD, 128)
        to = lax.broadcasted_iota(jnp.int32, shape, 1) + 128 * i
        by_y, rest = to // 96, lax.rem(to, 96)
        source_row = (rest // 12) * 96 + by_y * 12 + lax.rem(rest, 12)
        same = lax.broadcasted_iota(jnp.int32, shape, 0) == source_row
        order[:, 128 * i:128 * i + 128] = jnp.where(same, 1.0, 0.0).astype(BF16)
    def front(j, carry):
        x = frames[j].astype(F32)
        normed = layer_norm(x, gains[0:1, :]).astype(BF16)
        arrived, place = source(j)
        seq[0:EDGE, :] = jnp.where(arrived, e_arr[place], e_loc[j]).astype(F32)
        seq[EDGE:EDGE + FR, :] = normed.astype(F32)
        rows = pl.ds(pl.multiple_of(j * FR, FR), FR)
        for c in range(D // 128):
            lanes = slice(128 * c, 128 * c + 128)
            total = taps[0, :, lanes] * seq[0:FR, lanes]
            for t in range(1, KERNEL):
                total = total + taps[t, :, lanes] * seq[t:t + FR, lanes]
            mid[rows, lanes] = frames[j, :, lanes].astype(F32) + total
        second[rows, :] = layer_norm(mid[rows, :], gains[1:2, :]).astype(BF16)
        return carry

    def serve(rings, h, k, roles=(0, 1)):
        for role in roles:
            @pl.when(core == role)
            def _():
                rings[role].serve(h, k)

    def front_two(i):
        lax.fori_loop(2 * i, 2 * i + 2, front, 0)

    serve(ring_q, 0, 1)
    serve(ring_q, 1, 1)
    for r in range(4):
        book.arrive(None, lambda: copy_e(r), ("e", r))
    front_two(0)
    front_two(1)

    def compact(role):
        spread_o[role].arrive(0)
        for p in range(RING):
            tmp_o[12 * p:12 * p + 12, :] = p1o[p].astype(F32)
        for h in range(2):
            lanes = slice(PART * h, PART * h + PART)
            bufo[role, h, across[role]] = tmp_o[:, lanes].astype(BF16)
            ring_o[role].start(h)

    serve(ring_q, 0, 2)
    by_role(compact)
    front_two(2)
    serve(ring_q, 1, 2)
    front_two(3)
    serve(ring_q, 0, 3)
    front_two(4)
    serve(ring_q, 1, 3)
    front_two(5)
    serve(ring_o, 0, 1)
    serve(ring_o, 1, 1)
    serve(ring_q, 0, 4, (1,))
    serve(ring_q, 1, 4, (1,))

    def project(role, h):
        @pl.when(core == 1 - role)
        def _():
            ring_q[role].shared(1 - role, (h,))

        n = WIDTHS[role] // 2
        total = jnp.zeros((SLOTS * FR, n), F32)
        for g in range(4):
            part = bufq[role][h, 2 * g:2 * g + 2].astype(F32).reshape(384, n)
            total = total + jnp.dot(
                second[:, 384 * g:384 * g + 384], part.astype(BF16),
                preferred_element_type=F32,
            )
        for m in range(0, n, PART):
            to = STARTS[role] + 2 * m + PART * h
            proj[:, to:to + PART] = total[:, m:m + PART].astype(BF16)

    project(1, 0)
    project(1, 1)
    serve(ring_q, 0, 4, (0,))
    serve(ring_o, 0, 2)
    serve(ring_o, 1, 2)
    project(0, 0)
    serve(ring_q, 1, 4, (0,))
    serve(ring_o, 0, 3)
    serve(ring_o, 1, 3)
    project(0, 1)
    for r in range(4):
        book.arrive(None, lambda: copy_c(r), ("c", r))

    key_pos = lax.broadcasted_iota(jnp.int32, (HEADS * FR, CTX + FR), 1)
    frame = lax.rem(lax.broadcasted_iota(jnp.int32, (HEADS * FR, CTX + FR), 0), FR)

    def attend(group):
        rows = [slice(FR * j, FR * j + FR) for j in group]
        scores, values = [], []
        for j, at_rows in zip(group, rows):
            arrived, place = source(j)
            cached = jnp.where(arrived, c_arr[place], c_loc[j])
            keys = jnp.concatenate([cached[:, :HD], proj[at_rows, HD:2 * HD]], axis=0)
            values.append(
                jnp.concatenate([cached[:, HD:], proj[at_rows, 2 * HD:]], axis=0)
            )
            parts = []
            for n, ((low, high), (top, end)) in enumerate(zip(TILES, TILE_ROWS)):
                lanes = slice(256 * n, 256 * n + 256)
                q = jnp.concatenate([proj[at_rows, lanes]] * (high - low), axis=0)
                parts.append(lax.dot_general(
                    q * hmask[top:end, :], keys[:, lanes], (((1,), (1,)), ((), ())),
                    preferred_element_type=F32,
                ))
            s0, s1, s2 = parts
            scores.append(jnp.concatenate(
                [s0[:32], s0[32:] + s1[:16], s1[16:48], s1[48:] + s2[:16], s2[16:]], axis=0
            ) * HSIZE ** (-0.5))
        probs = []
        for j, score in zip(group, scores):
            allowed = ((key_pos < CTX) & (key_pos >= CTX - lengths[j])) | (
                (key_pos >= CTX) & (key_pos - CTX <= frame)
            )
            score = jnp.where(allowed, score, -1e30)
            weights = jnp.exp(score - jnp.max(score, axis=-1, keepdims=True))
            total = jnp.sum(weights, axis=-1, keepdims=True)
            probs.append((weights / total).astype(BF16))
        for at_rows, prob, value in zip(rows, probs, values):
            for n, ((low, high), (top, end)) in enumerate(zip(TILES, TILE_ROWS)):
                lanes = slice(256 * n, 256 * n + 256)
                wide = jnp.dot(
                    prob[FR * low:FR * high], value[:, lanes], preferred_element_type=F32
                ) * fmask[top:end, :]
                total = wide[0:FR]
                for hd in range(1, high - low):
                    total = total + wide[FR * hd:FR * hd + FR]
                ctx[at_rows, lanes] = total.astype(BF16)

    def hand(n):
        span = pl.ds(GROUP * n, GROUP)
        return remote(ostage.at[span], out.at[span], h_send, h_recv, n, next_sec)

    for n in range(SLOTS // GROUP):
        group = range(GROUP * n, GROUP * n + GROUP)
        attend(group)
        if n == 0:
            serve(ring_o, 0, 4)
            serve(ring_o, 1, 4)
            for role in range(2):
                @pl.when(core == 1 - role)
                def _():
                    ring_o[role].shared(1 - role)
        rows = slice(FR * GROUP * n, FR * GROUP * n + FR * GROUP)
        context = ctx[rows, :]
        turned = jnp.dot(context, order[...], preferred_element_type=F32).astype(BF16)
        for half in range(2):
            for part in range(2):
                at_lane = OH * half + PART * part
                lanes = slice(at_lane, at_lane + PART)
                weights = bufo[half, part].reshape(HD, PART)
                result = jnp.dot(
                    turned if half else context, weights, preferred_element_type=F32
                ) + mid[rows, lanes]
                for m, j in enumerate(group):
                    live = counts[0] > j
                    ostage[j, :, lanes] = jnp.where(
                        live, result[FR * m:FR * m + FR], 0.0
                    ).astype(BF16)
        book.start(None, lambda n=n: hand(n), ("h", n))

    by_role(book.close)
    book.close(None)
    for r in range(4):
        @pl.when(crossing[r])
        def _():
            book.close(("z", r))

        @pl.when(jnp.logical_not(crossing[r]))
        def _():
            book.close(("d", r))


def body(
    new_frames, conv_edges, kv_cache, norm_gains, conv_kernel,
    w_qkv, w_out, move_targets, lengths, counts,
):
    vmem = pl.BlockSpec(memory_space=pltpu.VMEM)
    smem = pl.BlockSpec(memory_space=pltpu.SMEM)
    any_ = pl.BlockSpec(memory_space=pl.ANY)
    dma = pltpu.SemaphoreType.DMA
    rows = SLOTS * FR
    out = pl.pallas_call(
        kernel,
        out_shape=jax.ShapeDtypeStruct((SLOTS, FR, D), BF16),
        in_specs=[any_, any_, any_, vmem, any_, any_, any_, smem, smem, smem],
        out_specs=any_,
        scratch_shapes=[
            pltpu.VMEM((SLOTS, FR, D), BF16),
            pltpu.VMEM((KERNEL, 1, D), F32),
            pltpu.VMEM((12, QW), BF16),
            pltpu.VMEM((6, D), BF16),
            pltpu.VMEM((SLOTS, EDGE, D), BF16),
            pltpu.VMEM((SLOTS, CTX, D), BF16),
            pltpu.VMEM((4, EDGE, D), BF16),
            pltpu.VMEM((4, CTX, D), BF16),
            pltpu.VMEM((4, EDGE, D), BF16),
            pltpu.VMEM((4, CTX, D), BF16),
            pltpu.VMEM((2, EDGE, D), BF16),
            pltpu.VMEM((2, CTX, D), BF16),
            pltpu.VMEM((12, WIDTHS[0]), BF16),
            pltpu.VMEM((12, WIDTHS[1]), BF16),
            pltpu.VMEM((6, OH), BF16),
            pltpu.VMEM((2, RING, RING, 24, WIDTHS[0] // 2), BF16),
            pltpu.VMEM((2, RING, RING, 24, WIDTHS[1] // 2), BF16),
            pltpu.VMEM((RING, 12, OH), BF16),
            pltpu.VMEM((2, 2, RING, 96, PART), BF16),
            pltpu.VMEM((24, WIDTHS[0] // 2), F32),
            pltpu.VMEM((96, OH), F32),
            pltpu.VMEM((48, D), F32),
            pltpu.VMEM((rows, D), F32),
            pltpu.VMEM((rows, D), BF16),
            pltpu.VMEM((rows, QW), BF16),
            pltpu.VMEM((rows, HD), BF16),
            pltpu.VMEM((160, 256), BF16),
            pltpu.VMEM((160, 256), F32),
            pltpu.VMEM((HD, HD), BF16),
            pltpu.VMEM((SLOTS, FR, D), BF16),
            dma((6,)), dma((2,)), dma((2,)), dma((8,)), dma((8,)),
            dma((16,)), dma((16,)), dma((8,)), dma((8,)),
            dma((16,)), dma((16,)), dma((16,)), dma((16,)),
            dma((18,)), dma((18,)), dma((18,)), dma((18,)),
            dma((4,)), dma((4,)), dma((4,)), dma((4,)),
        ],
        compiler_params=pltpu.CompilerParams(
            collective_id=0, has_side_effects=True, vmem_limit_bytes=56 * 2 ** 20
        ),
        cost_estimate=pl.CostEstimate(
            flops=2 * 10 ** 9, bytes_accessed=6 * 10 ** 6, transcendentals=10 ** 5
        ),
    )(
        new_frames[0], conv_edges[0], kv_cache[0], norm_gains[0], conv_kernel.transpose(1, 0, 2),
        w_qkv[0], w_out[0], move_targets, lengths, counts,
    )
    return out[None]


def solution(mesh):
    placed = (
        P("section", "sess", None, None),
        P("section", "sess", None, None),
        P("section", "sess", None, None),
        P("section", None, None),
        P("section", None, None),
        P("section", "sess", None),
        P("section", "sess", None),
        P("sess"),
        P("sess"),
        P("sess"),
    )
    return jax.shard_map(
        body,
        mesh=mesh,
        in_specs=placed,
        out_specs=P("section", "sess", None, None),
        check_vma=False,
    )
```

```python
import functools

import jax
import jax.numpy as jnp
from jax import lax
from jax.experimental import pallas as pl
from jax.experimental.pallas import tpu as pltpu
from jax.sharding import PartitionSpec as P

D = 1536
HEADS = 8
HSIZE = 96
HD = 768
KERNEL = 31
EDGE = 30
CTX = 64
FR = 16
SLOTS = 12
RING = 8
N_SESS = 128
QW = 3 * HD
OH = D // 2
WIDTHS = (2 * HD, HD)
STARTS = (0, 2 * HD)
PART = HD // 2
GROUP = 4
LAST = RING - 1
TILES = ((0, 3), (2, 6), (5, 8))
TILE_ROWS = ((0, 48), (48, 112), (112, 160))
OFFSETS = (1, -1, 2, -2)
MESH = pl.DeviceIdType.MESH
F32 = jnp.float32
BF16 = jnp.bfloat16


class Book:
    def __init__(self):
        self.started, self.arrived, self.left = {}, set(), set()

    def start(self, role, make, key):
        make().start()
        self.started[(role, key)] = make

    def arrive(self, role, make, key):
        make().wait_recv()
        self.arrived.add((role, key))

    def sent(self, role, key):
        self.started[(role, key)]().wait_send()
        self.left.add((role, key))

    def close(self, role):
        for key, make in self.started.items():
            if key[0] == role and key not in self.left:
                make().wait_send()
            if key[0] == role and key not in self.arrived:
                make().wait_recv()


def hops(d, h):
    return 4 if d == h else 3


def turn(me, by):
    return lax.rem(me + (by % RING), RING)


def every_share():
    out = [(0, 0, 0), (0, 1, 0)]
    for d in range(2):
        for h in range(2):
            for k in range(1, hops(d, h) + 1):
                out.append((d, h, k))
    return out


def remote(src, dst, send, recv, i, dev):
    return pltpu.make_async_remote_copy(
        src_ref=src,
        dst_ref=dst,
        send_sem=send.at[i],
        recv_sem=recv.at[i],
        device_id=dev,
        device_id_type=MESH,
    )


class Spread:
    def __init__(self, book, role, name, slot, me, ids, sems):
        self.book, self.role, self.name = book, role, name
        self.slot, self.me, self.ids, self.sems = slot, me, ids, sems

    def copy(self, d, h, back):
        ref = self.slot(turn(self.me, back), h)
        return remote(ref, ref, *self.sems, 8 * h + d - 1, self.ids(d))

    def start(self, h):
        for d in (1, 7, 2, 6, 3, 5, 4):
            make = lambda d=d: self.copy(d, h, 0)
            self.book.start(self.role, make, (self.name, d, h))

    def arrive(self, h):
        for d in (1, 7, 2, 6, 3, 5, 4):
            self.book.arrive(self.role, lambda: self.copy(d, h, -d), (self.name, d, h))


class Ring:
    def __init__(self, book, role, name, slot, me, place, away, sib, sems, share_sems):
        self.book, self.role, self.name = book, role, name
        self.slot, self.me, self.place, self.away = slot, me, place, away
        self.sib, self.sems, self.share_sems = sib, sems, share_sems

    def group(self, d, k):
        return turn(self.me, -k if d == 0 else k)

    def copy(self, d, h, k, back):
        ref = self.slot(self.group(d, k - back), h)
        to = self.place(turn(self.me, 1 - 2 * d))
        return remote(ref, ref, *self.sems, (d * 2 + h) * 4 + k - 1, to)

    def last(self, h, back):
        away = self.away[h]
        group = lax.rem(self.me + 5 + 6 * away, RING) if back else turn(self.me, 4)
        ref = self.slot(group, h)
        to = self.place(lax.rem(self.me + 1 + 6 * away, RING))
        return remote(ref, ref, *self.sems, 12 * h + 3, to)

    def share(self, d, h, k):
        ref = self.slot(self.group(d, k), h)
        i = h if k == 0 else 2 + (d * 2 + h) * 4 + k - 1
        return remote(ref, ref, *self.share_sems, i, self.sib)

    def pass_on(self, d, h, k):
        make = lambda: self.copy(d, h, k + 1, 1)
        self.book.start(self.role, make, (self.name, d, h, k + 1))

    def give(self, d, h, k):
        self.book.start(self.role, lambda: self.share(d, h, k), (self.name, "s", d, h, k))

    def start(self, h):
        for d in (h, 1 - h):
            self.pass_on(d, h, 0)
        self.give(0, h, 0)

    def serve(self, h, k):
        if k == 4:
            self.book.arrive(self.role, lambda: self.last(h, 0), (self.name, h, h, 4))
            self.give(h, h, 4)
            return
        for d in (h, 1 - h):
            self.book.arrive(self.role, lambda: self.copy(d, h, k, 0), (self.name, d, h, k))
            if k < 3:
                self.pass_on(d, h, k)
                self.give(d, h, k)
        if k == 3:
            make = lambda: self.last(h, 1)
            self.book.start(self.role, make, (self.name, h, h, 4))
            for d in (h, 1 - h):
                self.give(d, h, k)

    def shared(self, book_role, parts=(0, 1)):
        for d, h, k in every_share():
            if h in parts:
                self.book.arrive(book_role, lambda: self.share(d, h, k), (self.name, "s", d, h, k))


def layer_norm(values, gain):
    center = values - jnp.mean(values, axis=-1, keepdims=True)
    spread = jnp.mean(center * center, axis=-1, keepdims=True)
    return center * lax.rsqrt(spread + 1e-05) * gain


def kernel(
    frames_in, edges, cache, gains, taps_in, wq_in, wo_in, targets, lengths, counts,
    out,
    frames, taps, wq, wo,
    e_loc, c_loc, e_stage, c_stage, e_arr, c_arr, e_via, c_via,
    x_q0, x_q1, x_o, bufq0, bufq1, p1o, bufo,
    tmp_q, tmp_o, seq, mid, second, proj, ctx, hmask, fmask, order, ostage,
    loc_sem, x_send, x_recv, m_send, m_recv,
    pq_send, pq_recv, po_send, po_recv,
    qq_send, qq_recv, qo_send, qo_recv,
    sq_send, sq_recv, so_send, so_recv,
    h_send, h_recv, v_send, v_recv,
):
    sess = lax.axis_index("sess")
    sec = lax.axis_index("section")
    nsec = lax.axis_size("section")
    core = lax.rem(sess, 2)
    y = lax.rem(sess // 2, RING)
    z = sess // (2 * RING)
    book = Book()

    def at(zz, yy, cc):
        return ((zz * RING + yy) * 2 + cc, sec)

    def on_y(d):
        return at(z, turn(y, d), core)

    def on_z(d):
        return at(turn(z, d), y, core)

    sib = at(z, y, 1 - core)
    next_sec = (sess, lax.rem(sec + 1, nsec))
    prev_sec = (sess, lax.rem(sec + nsec - 1, nsec))
    moves = [(lax.rem(sess + N_SESS + o, N_SESS), sec) for o in OFFSETS]
    bufq = (bufq0, bufq1)
    x_q = (x_q0, x_q1)

    def by_role(fn):
        for role in range(2):
            @pl.when(core == role)
            def _():
                fn(role)

    barrier = pltpu.get_barrier_semaphore()
    greet = [*moves, sib, next_sec, prev_sec, at(z, LAST - y, 1 - core)]
    greet += [on_y(d) for d in range(1, RING)] + [on_z(d) for d in range(1, RING)]
    for dev in greet:
        pl.semaphore_signal(barrier, inc=1, device_id=dev, device_id_type=MESH)

    loads = [
        pltpu.make_async_copy(src, dst, loc_sem.at[i])
        for i, (src, dst) in enumerate(
            ((wq_in, wq), (wo_in, wo), (edges, e_loc), (cache, c_loc),
             (frames_in, frames), (taps_in, taps))
        )
    ]
    for load in loads:
        load.start()

    wanted = [m[0] * SLOTS for m in moves]

    def hits(j):
        t = targets[j]
        return [(t >= w) & (t < w + SLOTS) for w in wanted]

    picks = [jnp.int32(0)] * 4
    for j in range(SLOTS):
        picks = [jnp.where(hit, jnp.int32(j), p) for hit, p in zip(hits(j), picks)]

    def source(j):
        found = hits(j)
        arrived = found[0] | found[1] | found[2] | found[3]
        place = jnp.int32(0)
        for r in range(1, 4):
            place = jnp.where(found[r], jnp.int32(r), place)
        return arrived, place

    for load in loads[:3]:
        load.wait()
    pl.semaphore_wait(barrier, len(greet))

    def swap_q(dst_role):
        return remote(
            wq.at[:, pl.ds(STARTS[dst_role], WIDTHS[dst_role])],
            x_q[dst_role], x_send, x_recv, 0, sib,
        )

    def swap_o(role):
        return remote(wo.at[:, pl.ds((1 - role) * OH, OH)], x_o, x_send, x_recv, 1, sib)

    def start_swap(role):
        book.start(role, lambda: swap_q(1 - role), "xq")
        book.start(role, lambda: swap_o(role), "xo")

    by_role(start_swap)

    def copy_e(r):
        return remote(e_stage.at[r], e_arr.at[r], m_send, m_recv, r, moves[r])

    def copy_c(r):
        return remote(c_stage.at[r], c_arr.at[r], m_send, m_recv, 4 + r, moves[r])

    crossing = [(y == LAST) & (core == 1), (y == 0) & (core == 0), y == LAST, y == 0]
    parts = ((e_stage, e_via, e_arr), (c_stage, c_via, c_arr))

    def across_z(m, r):
        stage, via, _ = parts[m]
        i = 2 * m + r // 2
        return remote(
            stage.at[r], via.at[r // 2], v_send, v_recv, i, on_z(1 if r % 2 == 0 else -1)
        )

    def along_y(m, r):
        _, via, arr = parts[m]
        to = at(z, LAST - y, core if r >= 2 else 1 - core)
        return remote(via.at[r // 2], arr.at[r], m_send, m_recv, 4 * m + r, to)

    def leave_row(m):
        for r in range(4):
            @pl.when(crossing[r])
            def _():
                book.start(("z", r), lambda r=r: across_z(m, r), ("z", m))

    def leave(m):
        for r in range(4):
            @pl.when(jnp.logical_not(crossing[r]))
            def _():
                book.start(("d", r), lambda r=r: (copy_e, copy_c)[m](r), ("d", m))
                book.arrived.add((("d", r), ("d", m)))

    def pass_along(m):
        for r in range(4):
            @pl.when(crossing[r])
            def _():
                book.arrive(("z", r), lambda r=r: across_z(m, r), ("z", m))
                book.start(("z", r), lambda r=r: along_y(m, r), ("y", m))
                book.arrived.add((("z", r), ("y", m)))

    for r in range(4):
        e_stage[r] = e_loc[picks[r]]
    leave_row(0)
    loads[3].wait()
    for r in range(4):
        c_stage[r] = c_loc[picks[r]]
    leave_row(1)

    def q_block(role):
        if role == 0:
            return lambda g, h: bufq0.at[h, z, g]
        return lambda g, h: bufq1.at[h, g, y]

    def q_group(role):
        if role == 0:
            return lambda g, h: bufq0.at[h, g]
        return lambda g, h: bufq1.at[h, :, g]

    along, across = (y, z), (z, y)
    on_along = (on_y, on_z)
    across_at = (lambda v: at(v, y, core), lambda v: at(z, v, core))
    away = ((0, 1), (0, 1))
    spread_q = [
        Spread(book, role, "pq", q_block(role), along[role], on_along[role],
               (pq_send, pq_recv))
        for role in range(2)
    ]
    ring_q = [
        Ring(book, role, "qq", q_group(role), across[role], across_at[role], away[role], sib,
             (qq_send, qq_recv), (sq_send, sq_recv))
        for role in range(2)
    ]
    spread_o = [
        Spread(book, role, "po", lambda g, h: p1o.at[g], along[role], on_along[role],
               (po_send, po_recv))
        for role in range(2)
    ]
    ring_o = [
        Ring(book, role, "qo", lambda g, h, role=role: bufo.at[role, h, g], across[role],
             across_at[role], away[role], sib, (qo_send, qo_recv), (so_send, so_recv))
        for role in range(2)
    ]

    def joined(role, n, own, other):
        first, last = (own, other) if role == 0 else (other, own)
        return first.astype(F32), last.astype(F32)

    def enter_q(role):
        book.arrive(role, lambda: swap_q(role), "xq")
        width = WIDTHS[role] // 2
        for h in range(2):
            for m in range(0, width, PART):
                lanes = slice(2 * m + PART * h, 2 * m + PART * h + PART)
                own = wq[:, STARTS[role] + lanes.start:STARTS[role] + lanes.stop]
                first, last = joined(role, 12, own, x_q[role][:, lanes])
                tmp_q[0:12, m:m + PART] = first
                tmp_q[12:24, m:m + PART] = last
            bufq[role][h, z, y] = tmp_q[:, 0:width].astype(BF16)
            spread_q[role].start(h)

    by_role(enter_q)
    leave(0)

    def enter_o(role):
        book.arrive(role, lambda: swap_o(role), "xo")
        first, last = joined(role, 6, wo[:, role * OH:(role + 1) * OH], x_o[...])
        tmp_o[0:6, :] = first
        tmp_o[6:12, :] = last
        p1o[along[role]] = tmp_o[0:12, :].astype(BF16)

    by_role(enter_o)

    for (low, high), (top, end) in zip(TILES, TILE_ROWS):
        shape = (end - top, 256)
        head = lax.broadcasted_iota(jnp.int32, shape, 0) // FR + low
        lane = lax.broadcasted_iota(jnp.int32, shape, 1) + 256 * TILES.index((low, high))
        inside = (lane >= head * HSIZE) & (lane < head * HSIZE + HSIZE)
        fmask[top:end, :] = jnp.where(inside, 1.0, 0.0)
        hmask[top:end, :] = jnp.where(inside, 1.0, 0.0).astype(BF16)
    for load in loads[4:]:
        load.wait()

    def start_q(role):
        for h in range(2):
            spread_q[role].arrive(h)
            ring_q[role].start(h)
        spread_o[role].start(0)

    by_role(start_q)
    pass_along(0)

    for i in range(HD // 128):
        shape = (HD, 128)
        to = lax.broadcasted_iota(jnp.int32, shape, 1) + 128 * i
        by_y, rest = to // 96, lax.rem(to, 96)
        source_row = (rest // 12) * 96 + by_y * 12 + lax.rem(rest, 12)
        same = lax.broadcasted_iota(jnp.int32, shape, 0) == source_row
        order[:, 128 * i:128 * i + 128] = jnp.where(same, 1.0, 0.0).astype(BF16)
    def front(j, carry):
        x = frames[j].astype(F32)
        normed = layer_norm(x, gains[0:1, :]).astype(BF16)
        arrived, place = source(j)
        seq[0:EDGE, :] = jnp.where(arrived, e_arr[place], e_loc[j]).astype(F32)
        seq[EDGE:EDGE + FR, :] = normed.astype(F32)
        rows = pl.ds(pl.multiple_of(j * FR, FR), FR)
        for c in range(D // 128):
            lanes = slice(128 * c, 128 * c + 128)
            total = taps[0, :, lanes] * seq[0:FR, lanes]
            for t in range(1, KERNEL):
                total = total + taps[t, :, lanes] * seq[t:t + FR, lanes]
            mid[rows, lanes] = frames[j, :, lanes].astype(F32) + total
        second[rows, :] = layer_norm(mid[rows, :], gains[1:2, :]).astype(BF16)
        return carry

    def serve(rings, h, k, roles=(0, 1)):
        for role in roles:
            @pl.when(core == role)
            def _():
                rings[role].serve(h, k)

    def front_two(i):
        lax.fori_loop(2 * i, 2 * i + 2, front, 0)

    serve(ring_q, 0, 1)
    serve(ring_q, 1, 1)
    leave(1)
    pass_along(1)
    for r in range(4):
        book.arrive(None, lambda: copy_e(r), ("e", r))
    def compact(role):
        spread_o[role].arrive(0)
        for p in range(RING):
            tmp_o[12 * p:12 * p + 12, :] = p1o[p].astype(F32)
        for h in range(2):
            lanes = slice(PART * h, PART * h + PART)
            bufo[role, h, across[role]] = tmp_o[:, lanes].astype(BF16)
            ring_o[role].start(h)

    by_role(compact)
    front_two(0)
    front_two(1)

    serve(ring_q, 0, 2)
    front_two(2)
    serve(ring_q, 1, 2)
    front_two(3)
    serve(ring_q, 0, 3)
    front_two(4)
    serve(ring_q, 1, 3)
    front_two(5)
    serve(ring_o, 0, 1)
    serve(ring_o, 1, 1)
    serve(ring_q, 0, 4, (1,))
    serve(ring_q, 1, 4, (1,))

    def project(role, h):
        @pl.when(core == 1 - role)
        def _():
            ring_q[role].shared(1 - role, (h,))

        n = WIDTHS[role] // 2
        total = jnp.zeros((SLOTS * FR, n), F32)
        for g in range(4):
            part = bufq[role][h, 2 * g:2 * g + 2].astype(F32).reshape(384, n)
            total = total + jnp.dot(
                second[:, 384 * g:384 * g + 384], part.astype(BF16),
                preferred_element_type=F32,
            )
        for m in range(0, n, PART):
            to = STARTS[role] + 2 * m + PART * h
            proj[:, to:to + PART] = total[:, m:m + PART].astype(BF16)

    project(1, 0)
    project(1, 1)
    serve(ring_q, 0, 4, (0,))
    serve(ring_o, 0, 2)
    serve(ring_o, 1, 2)
    project(0, 0)
    serve(ring_q, 1, 4, (0,))
    serve(ring_o, 0, 3)
    serve(ring_o, 1, 3)
    project(0, 1)
    for r in range(4):
        book.arrive(None, lambda: copy_c(r), ("c", r))

    key_pos = lax.broadcasted_iota(jnp.int32, (HEADS * FR, CTX + FR), 1)
    frame = lax.rem(lax.broadcasted_iota(jnp.int32, (HEADS * FR, CTX + FR), 0), FR)

    def attend(group):
        rows = [slice(FR * j, FR * j + FR) for j in group]
        scores, values = [], []
        for j, at_rows in zip(group, rows):
            arrived, place = source(j)
            cached = jnp.where(arrived, c_arr[place], c_loc[j])
            keys = jnp.concatenate([cached[:, :HD], proj[at_rows, HD:2 * HD]], axis=0)
            values.append(
                jnp.concatenate([cached[:, HD:], proj[at_rows, 2 * HD:]], axis=0)
            )
            parts = []
            for n, ((low, high), (top, end)) in enumerate(zip(TILES, TILE_ROWS)):
                lanes = slice(256 * n, 256 * n + 256)
                q = jnp.concatenate([proj[at_rows, lanes]] * (high - low), axis=0)
                parts.append(lax.dot_general(
                    q * hmask[top:end, :], keys[:, lanes], (((1,), (1,)), ((), ())),
                    preferred_element_type=F32,
                ))
            s0, s1, s2 = parts
            scores.append(jnp.concatenate(
                [s0[:32], s0[32:] + s1[:16], s1[16:48], s1[48:] + s2[:16], s2[16:]], axis=0
            ) * HSIZE ** (-0.5))
        probs = []
        for j, score in zip(group, scores):
            allowed = ((key_pos < CTX) & (key_pos >= CTX - lengths[j])) | (
                (key_pos >= CTX) & (key_pos - CTX <= frame)
            )
            score = jnp.where(allowed, score, -1e30)
            weights = jnp.exp(score - jnp.max(score, axis=-1, keepdims=True))
            total = jnp.sum(weights, axis=-1, keepdims=True)
            probs.append((weights / total).astype(BF16))
        for at_rows, prob, value in zip(rows, probs, values):
            for n, ((low, high), (top, end)) in enumerate(zip(TILES, TILE_ROWS)):
                lanes = slice(256 * n, 256 * n + 256)
                wide = jnp.dot(
                    prob[FR * low:FR * high], value[:, lanes], preferred_element_type=F32
                ) * fmask[top:end, :]
                total = wide[0:FR]
                for hd in range(1, high - low):
                    total = total + wide[FR * hd:FR * hd + FR]
                ctx[at_rows, lanes] = total.astype(BF16)

    def hand(n):
        span = pl.ds(GROUP * n, GROUP)
        return remote(ostage.at[span], out.at[span], h_send, h_recv, n, next_sec)

    for n in range(SLOTS // GROUP):
        group = range(GROUP * n, GROUP * n + GROUP)
        attend(group)
        if n == 0:
            serve(ring_o, 0, 4)
            serve(ring_o, 1, 4)
            for role in range(2):
                @pl.when(core == 1 - role)
                def _():
                    ring_o[role].shared(1 - role)
        rows = slice(FR * GROUP * n, FR * GROUP * n + FR * GROUP)
        context = ctx[rows, :]
        turned = jnp.dot(context, order[...], preferred_element_type=F32).astype(BF16)
        for half in range(2):
            for part in range(2):
                at_lane = OH * half + PART * part
                lanes = slice(at_lane, at_lane + PART)
                weights = bufo[half, part].reshape(HD, PART)
                result = jnp.dot(
                    turned if half else context, weights, preferred_element_type=F32
                ) + mid[rows, lanes]
                for m, j in enumerate(group):
                    live = counts[0] > j
                    ostage[j, :, lanes] = jnp.where(
                        live, result[FR * m:FR * m + FR], 0.0
                    ).astype(BF16)
        book.start(None, lambda n=n: hand(n), ("h", n))

    by_role(book.close)
    book.close(None)
    for r in range(4):
        @pl.when(crossing[r])
        def _():
            book.close(("z", r))

        @pl.when(jnp.logical_not(crossing[r]))
        def _():
            book.close(("d", r))


def body(
    new_frames, conv_edges, kv_cache, norm_gains, conv_kernel,
    w_qkv, w_out, move_targets, lengths, counts,
):
    vmem = pl.BlockSpec(memory_space=pltpu.VMEM)
    smem = pl.BlockSpec(memory_space=pltpu.SMEM)
    any_ = pl.BlockSpec(memory_space=pl.ANY)
    dma = pltpu.SemaphoreType.DMA
    rows = SLOTS * FR
    out = pl.pallas_call(
        kernel,
        out_shape=jax.ShapeDtypeStruct((SLOTS, FR, D), BF16),
        in_specs=[any_, any_, any_, vmem, any_, any_, any_, smem, smem, smem],
        out_specs=any_,
        scratch_shapes=[
            pltpu.VMEM((SLOTS, FR, D), BF16),
            pltpu.VMEM((KERNEL, 1, D), F32),
            pltpu.VMEM((12, QW), BF16),
            pltpu.VMEM((6, D), BF16),
            pltpu.VMEM((SLOTS, EDGE, D), BF16),
            pltpu.VMEM((SLOTS, CTX, D), BF16),
            pltpu.VMEM((4, EDGE, D), BF16),
            pltpu.VMEM((4, CTX, D), BF16),
            pltpu.VMEM((4, EDGE, D), BF16),
            pltpu.VMEM((4, CTX, D), BF16),
            pltpu.VMEM((2, EDGE, D), BF16),
            pltpu.VMEM((2, CTX, D), BF16),
            pltpu.VMEM((12, WIDTHS[0]), BF16),
            pltpu.VMEM((12, WIDTHS[1]), BF16),
            pltpu.VMEM((6, OH), BF16),
            pltpu.VMEM((2, RING, RING, 24, WIDTHS[0] // 2), BF16),
            pltpu.VMEM((2, RING, RING, 24, WIDTHS[1] // 2), BF16),
            pltpu.VMEM((RING, 12, OH), BF16),
            pltpu.VMEM((2, 2, RING, 96, PART), BF16),
            pltpu.VMEM((24, WIDTHS[0] // 2), F32),
            pltpu.VMEM((96, OH), F32),
            pltpu.VMEM((48, D), F32),
            pltpu.VMEM((rows, D), F32),
            pltpu.VMEM((rows, D), BF16),
            pltpu.VMEM((rows, QW), BF16),
            pltpu.VMEM((rows, HD), BF16),
            pltpu.VMEM((160, 256), BF16),
            pltpu.VMEM((160, 256), F32),
            pltpu.VMEM((HD, HD), BF16),
            pltpu.VMEM((SLOTS, FR, D), BF16),
            dma((6,)), dma((2,)), dma((2,)), dma((8,)), dma((8,)),
            dma((16,)), dma((16,)), dma((8,)), dma((8,)),
            dma((16,)), dma((16,)), dma((16,)), dma((16,)),
            dma((18,)), dma((18,)), dma((18,)), dma((18,)),
            dma((4,)), dma((4,)), dma((4,)), dma((4,)),
        ],
        compiler_params=pltpu.CompilerParams(
            collective_id=0, has_side_effects=True, vmem_limit_bytes=56 * 2 ** 20
        ),
        cost_estimate=pl.CostEstimate(
            flops=2 * 10 ** 9, bytes_accessed=6 * 10 ** 6, transcendentals=10 ** 5
        ),
    )(
        new_frames[0], conv_edges[0], kv_cache[0], norm_gains[0], conv_kernel.transpose(1, 0, 2),
        w_qkv[0], w_out[0], move_targets, lengths, counts,
    )
    return out[None]


def solution(mesh):
    placed = (
        P("section", "sess", None, None),
        P("section", "sess", None, None),
        P("section", "sess", None, None),
        P("section", None, None),
        P("section", None, None),
        P("section", "sess", None),
        P("section", "sess", None),
        P("sess"),
        P("sess"),
        P("sess"),
    )
    return jax.shard_map(
        body,
        mesh=mesh,
        in_specs=placed,
        out_specs=P("section", "sess", None, None),
        check_vma=False,
    )
```

```python
import functools

import jax
import jax.numpy as jnp
from jax import lax
from jax.experimental import pallas as pl
from jax.experimental.pallas import tpu as pltpu
from jax.sharding import PartitionSpec as P

D = 1536
HEADS = 8
HSIZE = 96
HD = 768
KERNEL = 31
EDGE = 30
CTX = 64
FR = 16
SLOTS = 12
RING = 8
N_SESS = 128
QW = 3 * HD
OH = D // 2
WIDTHS = (2 * HD, HD)
STARTS = (0, 2 * HD)
PART = HD // 2
GROUP = 4
LAST = RING - 1
TILES = ((0, 3), (2, 6), (5, 8))
TILE_ROWS = ((0, 48), (48, 112), (112, 160))
OFFSETS = (1, -1, 2, -2)
MESH = pl.DeviceIdType.MESH
F32 = jnp.float32
BF16 = jnp.bfloat16


class Book:
    def __init__(self):
        self.started, self.arrived, self.left = {}, set(), set()

    def start(self, role, make, key):
        make().start()
        self.started[(role, key)] = make

    def arrive(self, role, make, key):
        make().wait_recv()
        self.arrived.add((role, key))

    def sent(self, role, key):
        self.started[(role, key)]().wait_send()
        self.left.add((role, key))

    def close(self, role):
        for key, make in self.started.items():
            if key[0] == role and key not in self.left:
                make().wait_send()
            if key[0] == role and key not in self.arrived:
                make().wait_recv()


def hops(d, h):
    return 4 if d == h else 3


def turn(me, by):
    return lax.rem(me + (by % RING), RING)


def every_share():
    out = [(0, 0, 0), (0, 1, 0)]
    for d in range(2):
        for h in range(2):
            for k in range(1, hops(d, h) + 1):
                out.append((d, h, k))
    return out


def remote(src, dst, send, recv, i, dev):
    return pltpu.make_async_remote_copy(
        src_ref=src,
        dst_ref=dst,
        send_sem=send.at[i],
        recv_sem=recv.at[i],
        device_id=dev,
        device_id_type=MESH,
    )


class Spread:
    def __init__(self, book, role, name, slot, me, ids, sems):
        self.book, self.role, self.name = book, role, name
        self.slot, self.me, self.ids, self.sems = slot, me, ids, sems

    def copy(self, d, h, back):
        ref = self.slot(turn(self.me, back), h)
        return remote(ref, ref, *self.sems, 8 * h + d - 1, self.ids(d))

    def start(self, h):
        for d in (1, 7, 2, 6, 3, 5, 4):
            make = lambda d=d: self.copy(d, h, 0)
            self.book.start(self.role, make, (self.name, d, h))

    def arrive(self, h):
        for d in (1, 7, 2, 6, 3, 5, 4):
            self.book.arrive(self.role, lambda: self.copy(d, h, -d), (self.name, d, h))


class Ring:
    def __init__(self, book, role, name, slot, me, place, away, sib, sems, share_sems):
        self.book, self.role, self.name = book, role, name
        self.slot, self.me, self.place, self.away = slot, me, place, away
        self.sib, self.sems, self.share_sems = sib, sems, share_sems

    def group(self, d, k):
        return turn(self.me, -k if d == 0 else k)

    def copy(self, d, h, k, back):
        ref = self.slot(self.group(d, k - back), h)
        to = self.place(turn(self.me, 1 - 2 * d))
        return remote(ref, ref, *self.sems, (d * 2 + h) * 4 + k - 1, to)

    def last(self, h, back):
        away = self.away[h]
        group = lax.rem(self.me + 5 + 6 * away, RING) if back else turn(self.me, 4)
        ref = self.slot(group, h)
        to = self.place(lax.rem(self.me + 1 + 6 * away, RING))
        return remote(ref, ref, *self.sems, 12 * h + 3, to)

    def share(self, d, h, k):
        ref = self.slot(self.group(d, k), h)
        i = h if k == 0 else 2 + (d * 2 + h) * 4 + k - 1
        return remote(ref, ref, *self.share_sems, i, self.sib)

    def pass_on(self, d, h, k):
        make = lambda: self.copy(d, h, k + 1, 1)
        self.book.start(self.role, make, (self.name, d, h, k + 1))

    def give(self, d, h, k):
        self.book.start(self.role, lambda: self.share(d, h, k), (self.name, "s", d, h, k))

    def start(self, h):
        for d in (h, 1 - h):
            self.pass_on(d, h, 0)
        self.give(0, h, 0)

    def serve(self, h, k):
        if k == 4:
            self.book.arrive(self.role, lambda: self.last(h, 0), (self.name, h, h, 4))
            self.give(h, h, 4)
            return
        for d in (h, 1 - h):
            self.book.arrive(self.role, lambda: self.copy(d, h, k, 0), (self.name, d, h, k))
            if k < 3:
                self.pass_on(d, h, k)
                self.give(d, h, k)
        if k == 3:
            make = lambda: self.last(h, 1)
            self.book.start(self.role, make, (self.name, h, h, 4))
            for d in (h, 1 - h):
                self.give(d, h, k)

    def shared(self, book_role, parts=(0, 1)):
        for d, h, k in every_share():
            if h in parts:
                self.book.arrive(book_role, lambda: self.share(d, h, k), (self.name, "s", d, h, k))


def layer_norm(values, gain):
    center = values - jnp.mean(values, axis=-1, keepdims=True)
    spread = jnp.mean(center * center, axis=-1, keepdims=True)
    return center * lax.rsqrt(spread + 1e-05) * gain


def kernel(
    frames_in, edges, cache, gains, taps_in, wq_in, wo_in, targets, lengths, counts,
    out,
    frames, taps, wq, wo,
    e_loc, c_loc, e_stage, c_stage, e_arr, c_arr, e_via, c_via,
    x_q0, x_q1, x_o, bufq0, bufq1, p1o, bufo,
    tmp_q, tmp_o, seq, mid, second, proj, ctx, hmask, fmask, order, ostage,
    loc_sem, x_send, x_recv, m_send, m_recv,
    pq_send, pq_recv, po_send, po_recv,
    qq_send, qq_recv, qo_send, qo_recv,
    sq_send, sq_recv, so_send, so_recv,
    h_send, h_recv, v_send, v_recv,
):
    sess = lax.axis_index("sess")
    sec = lax.axis_index("section")
    nsec = lax.axis_size("section")
    core = lax.rem(sess, 2)
    y = lax.rem(sess // 2, RING)
    z = sess // (2 * RING)
    book = Book()

    def at(zz, yy, cc):
        return ((zz * RING + yy) * 2 + cc, sec)

    def on_y(d):
        return at(z, turn(y, d), core)

    def on_z(d):
        return at(turn(z, d), y, core)

    sib = at(z, y, 1 - core)
    next_sec = (sess, lax.rem(sec + 1, nsec))
    prev_sec = (sess, lax.rem(sec + nsec - 1, nsec))
    moves = [(lax.rem(sess + N_SESS + o, N_SESS), sec) for o in OFFSETS]
    bufq = (bufq0, bufq1)
    x_q = (x_q0, x_q1)

    def by_role(fn):
        for role in range(2):
            @pl.when(core == role)
            def _():
                fn(role)

    barrier = pltpu.get_barrier_semaphore()
    greet = [*moves, sib, next_sec, prev_sec, at(z, LAST - y, 1 - core)]
    greet += [on_y(d) for d in range(1, RING)] + [on_z(d) for d in range(1, RING)]
    for dev in greet:
        pl.semaphore_signal(barrier, inc=1, device_id=dev, device_id_type=MESH)

    loads = [
        pltpu.make_async_copy(src, dst, loc_sem.at[i])
        for i, (src, dst) in enumerate(
            ((wq_in, wq), (wo_in, wo), (edges, e_loc), (cache, c_loc),
             (frames_in, frames), (taps_in, taps))
        )
    ]
    for load in loads:
        load.start()

    wanted = [m[0] * SLOTS for m in moves]

    def hits(j):
        t = targets[j]
        return [(t >= w) & (t < w + SLOTS) for w in wanted]

    picks = [jnp.int32(0)] * 4
    for j in range(SLOTS):
        picks = [jnp.where(hit, jnp.int32(j), p) for hit, p in zip(hits(j), picks)]

    def source(j):
        found = hits(j)
        arrived = found[0] | found[1] | found[2] | found[3]
        place = jnp.int32(0)
        for r in range(1, 4):
            place = jnp.where(found[r], jnp.int32(r), place)
        return arrived, place

    for load in loads[:3]:
        load.wait()
    pl.semaphore_wait(barrier, len(greet))

    def swap_q(dst_role):
        return remote(
            wq.at[:, pl.ds(STARTS[dst_role], WIDTHS[dst_role])],
            x_q[dst_role], x_send, x_recv, 0, sib,
        )

    def swap_o(role):
        return remote(wo.at[:, pl.ds((1 - role) * OH, OH)], x_o, x_send, x_recv, 1, sib)

    def start_swap(role):
        book.start(role, lambda: swap_q(1 - role), "xq")
        book.start(role, lambda: swap_o(role), "xo")

    by_role(start_swap)

    def copy_e(r):
        return remote(e_stage.at[r], e_arr.at[r], m_send, m_recv, r, moves[r])

    def copy_c(r):
        return remote(c_stage.at[r], c_arr.at[r], m_send, m_recv, 4 + r, moves[r])

    crossing = [(y == LAST) & (core == 1), (y == 0) & (core == 0), y == LAST, y == 0]
    parts = ((e_stage, e_via, e_arr), (c_stage, c_via, c_arr))

    def across_z(m, r):
        stage, via, _ = parts[m]
        i = 2 * m + r // 2
        return remote(
            stage.at[r], via.at[r // 2], v_send, v_recv, i, on_z(1 if r % 2 == 0 else -1)
        )

    def along_y(m, r):
        _, via, arr = parts[m]
        to = at(z, LAST - y, core if r >= 2 else 1 - core)
        return remote(via.at[r // 2], arr.at[r], m_send, m_recv, 4 * m + r, to)

    def leave_row(m):
        for r in range(4):
            @pl.when(crossing[r])
            def _():
                book.start(("z", r), lambda r=r: across_z(m, r), ("z", m))

    def leave(m):
        for r in range(4):
            @pl.when(jnp.logical_not(crossing[r]))
            def _():
                book.start(("d", r), lambda r=r: (copy_e, copy_c)[m](r), ("d", m))
                book.arrived.add((("d", r), ("d", m)))

    def pass_along(m):
        for r in range(4):
            @pl.when(crossing[r])
            def _():
                book.arrive(("z", r), lambda r=r: across_z(m, r), ("z", m))
                book.start(("z", r), lambda r=r: along_y(m, r), ("y", m))
                book.arrived.add((("z", r), ("y", m)))

    for r in range(4):
        e_stage[r] = e_loc[picks[r]]
    leave_row(0)
    loads[3].wait()
    for r in range(4):
        c_stage[r] = c_loc[picks[r]]
    leave_row(1)

    def q_block(role):
        if role == 0:
            return lambda g, h: bufq0.at[h, z, g]
        return lambda g, h: bufq1.at[h, g, y]

    def q_group(role):
        if role == 0:
            return lambda g, h: bufq0.at[h, g]
        return lambda g, h: bufq1.at[h, :, g]

    along, across = (y, z), (z, y)
    on_along = (on_y, on_z)
    across_at = (lambda v: at(v, y, core), lambda v: at(z, v, core))
    away = ((0, 1), (0, 1))
    spread_q = [
        Spread(book, role, "pq", q_block(role), along[role], on_along[role],
               (pq_send, pq_recv))
        for role in range(2)
    ]
    ring_q = [
        Ring(book, role, "qq", q_group(role), across[role], across_at[role], away[role], sib,
             (qq_send, qq_recv), (sq_send, sq_recv))
        for role in range(2)
    ]
    spread_o = [
        Spread(book, role, "po", lambda g, h: p1o.at[g], along[role], on_along[role],
               (po_send, po_recv))
        for role in range(2)
    ]
    ring_o = [
        Ring(book, role, "qo", lambda g, h, role=role: bufo.at[role, h, g], across[role],
             across_at[role], away[role], sib, (qo_send, qo_recv), (so_send, so_recv))
        for role in range(2)
    ]

    def joined(role, n, own, other):
        first, last = (own, other) if role == 0 else (other, own)
        return first.astype(F32), last.astype(F32)

    def enter_q(role):
        book.arrive(role, lambda: swap_q(role), "xq")
        width = WIDTHS[role] // 2
        for h in range(2):
            for m in range(0, width, PART):
                lanes = slice(2 * m + PART * h, 2 * m + PART * h + PART)
                own = wq[:, STARTS[role] + lanes.start:STARTS[role] + lanes.stop]
                first, last = joined(role, 12, own, x_q[role][:, lanes])
                tmp_q[0:12, m:m + PART] = first
                tmp_q[12:24, m:m + PART] = last
            bufq[role][h, z, y] = tmp_q[:, 0:width].astype(BF16)
            spread_q[role].start(h)

    by_role(enter_q)
    leave(0)

    def enter_o(role):
        book.arrive(role, lambda: swap_o(role), "xo")
        first, last = joined(role, 6, wo[:, role * OH:(role + 1) * OH], x_o[...])
        tmp_o[0:6, :] = first
        tmp_o[6:12, :] = last
        p1o[along[role]] = tmp_o[0:12, :].astype(BF16)

    by_role(enter_o)

    for (low, high), (top, end) in zip(TILES, TILE_ROWS):
        shape = (end - top, 256)
        head = lax.broadcasted_iota(jnp.int32, shape, 0) // FR + low
        lane = lax.broadcasted_iota(jnp.int32, shape, 1) + 256 * TILES.index((low, high))
        inside = (lane >= head * HSIZE) & (lane < head * HSIZE + HSIZE)
        fmask[top:end, :] = jnp.where(inside, 1.0, 0.0)
        hmask[top:end, :] = jnp.where(inside, 1.0, 0.0).astype(BF16)
    for load in loads[4:]:
        load.wait()

    def start_q(role):
        for h in range(2):
            spread_q[role].arrive(h)
            ring_q[role].start(h)
        spread_o[role].start(0)

    by_role(start_q)
    pass_along(0)

    for i in range(HD // 128):
        shape = (HD, 128)
        to = lax.broadcasted_iota(jnp.int32, shape, 1) + 128 * i
        by_y, rest = to // 96, lax.rem(to, 96)
        source_row = (rest // 12) * 96 + by_y * 12 + lax.rem(rest, 12)
        same = lax.broadcasted_iota(jnp.int32, shape, 0) == source_row
        order[:, 128 * i:128 * i + 128] = jnp.where(same, 1.0, 0.0).astype(BF16)
    def front(j, carry):
        x = frames[j].astype(F32)
        normed = layer_norm(x, gains[0:1, :]).astype(BF16)
        arrived, place = source(j)
        seq[0:EDGE, :] = jnp.where(arrived, e_arr[place], e_loc[j]).astype(F32)
        seq[EDGE:EDGE + FR, :] = normed.astype(F32)
        rows = pl.ds(pl.multiple_of(j * FR, FR), FR)
        for c in range(D // 128):
            lanes = slice(128 * c, 128 * c + 128)
            total = taps[0, :, lanes] * seq[0:FR, lanes]
            for t in range(1, KERNEL):
                total = total + taps[t, :, lanes] * seq[t:t + FR, lanes]
            mid[rows, lanes] = frames[j, :, lanes].astype(F32) + total
        second[rows, :] = layer_norm(mid[rows, :], gains[1:2, :]).astype(BF16)
        return carry

    def serve(rings, h, k, roles=(0, 1)):
        for role in roles:
            @pl.when(core == role)
            def _():
                rings[role].serve(h, k)

    def front_two(i):
        lax.fori_loop(2 * i, 2 * i + 2, front, 0)

    serve(ring_q, 0, 1)
    serve(ring_q, 1, 1)
    leave(1)
    pass_along(1)
    for r in range(4):
        book.arrive(None, lambda: copy_e(r), ("e", r))
    def compact(role):
        spread_o[role].arrive(0)
        for p in range(RING):
            tmp_o[12 * p:12 * p + 12, :] = p1o[p].astype(F32)
        for h in range(2):
            lanes = slice(PART * h, PART * h + PART)
            bufo[role, h, across[role]] = tmp_o[:, lanes].astype(BF16)
            ring_o[role].start(h)

    by_role(compact)
    front_two(0)
    front_two(1)

    serve(ring_q, 0, 2)
    front_two(2)
    serve(ring_q, 1, 2)
    front_two(3)
    serve(ring_q, 0, 3)
    serve(ring_o, 0, 1)
    serve(ring_o, 1, 1)
    front_two(4)
    serve(ring_q, 1, 3)
    serve(ring_o, 0, 2)
    serve(ring_o, 1, 2)
    front_two(5)
    serve(ring_q, 0, 4, (1,))
    serve(ring_q, 1, 4, (1,))

    def project(role, h):
        @pl.when(core == 1 - role)
        def _():
            ring_q[role].shared(1 - role, (h,))

        n = WIDTHS[role] // 2
        total = jnp.zeros((SLOTS * FR, n), F32)
        for g in range(4):
            part = bufq[role][h, 2 * g:2 * g + 2].astype(F32).reshape(384, n)
            total = total + jnp.dot(
                second[:, 384 * g:384 * g + 384], part.astype(BF16),
                preferred_element_type=F32,
            )
        for m in range(0, n, PART):
            to = STARTS[role] + 2 * m + PART * h
            proj[:, to:to + PART] = total[:, m:m + PART].astype(BF16)

    project(1, 0)
    project(1, 1)
    serve(ring_q, 0, 4, (0,))
    serve(ring_o, 0, 3)
    serve(ring_o, 1, 3)
    project(0, 0)
    serve(ring_q, 1, 4, (0,))
    project(0, 1)
    for r in range(4):
        book.arrive(None, lambda: copy_c(r), ("c", r))

    key_pos = lax.broadcasted_iota(jnp.int32, (HEADS * FR, CTX + FR), 1)
    frame = lax.rem(lax.broadcasted_iota(jnp.int32, (HEADS * FR, CTX + FR), 0), FR)

    def attend(group):
        rows = [slice(FR * j, FR * j + FR) for j in group]
        scores, values = [], []
        for j, at_rows in zip(group, rows):
            arrived, place = source(j)
            cached = jnp.where(arrived, c_arr[place], c_loc[j])
            keys = jnp.concatenate([cached[:, :HD], proj[at_rows, HD:2 * HD]], axis=0)
            values.append(
                jnp.concatenate([cached[:, HD:], proj[at_rows, 2 * HD:]], axis=0)
            )
            parts = []
            for n, ((low, high), (top, end)) in enumerate(zip(TILES, TILE_ROWS)):
                lanes = slice(256 * n, 256 * n + 256)
                q = jnp.concatenate([proj[at_rows, lanes]] * (high - low), axis=0)
                parts.append(lax.dot_general(
                    q * hmask[top:end, :], keys[:, lanes], (((1,), (1,)), ((), ())),
                    preferred_element_type=F32,
                ))
            s0, s1, s2 = parts
            scores.append(jnp.concatenate(
                [s0[:32], s0[32:] + s1[:16], s1[16:48], s1[48:] + s2[:16], s2[16:]], axis=0
            ) * HSIZE ** (-0.5))
        probs = []
        for j, score in zip(group, scores):
            allowed = ((key_pos < CTX) & (key_pos >= CTX - lengths[j])) | (
                (key_pos >= CTX) & (key_pos - CTX <= frame)
            )
            score = jnp.where(allowed, score, -1e30)
            weights = jnp.exp(score - jnp.max(score, axis=-1, keepdims=True))
            total = jnp.sum(weights, axis=-1, keepdims=True)
            probs.append((weights / total).astype(BF16))
        for at_rows, prob, value in zip(rows, probs, values):
            for n, ((low, high), (top, end)) in enumerate(zip(TILES, TILE_ROWS)):
                lanes = slice(256 * n, 256 * n + 256)
                wide = jnp.dot(
                    prob[FR * low:FR * high], value[:, lanes], preferred_element_type=F32
                ) * fmask[top:end, :]
                total = wide[0:FR]
                for hd in range(1, high - low):
                    total = total + wide[FR * hd:FR * hd + FR]
                ctx[at_rows, lanes] = total.astype(BF16)

    def hand(n):
        span = pl.ds(GROUP * n, GROUP)
        return remote(ostage.at[span], out.at[span], h_send, h_recv, n, next_sec)

    for n in range(SLOTS // GROUP):
        group = range(GROUP * n, GROUP * n + GROUP)
        attend(group)
        if n == 0:
            serve(ring_o, 0, 4)
            serve(ring_o, 1, 4)
            for role in range(2):
                @pl.when(core == 1 - role)
                def _():
                    ring_o[role].shared(1 - role)
        rows = slice(FR * GROUP * n, FR * GROUP * n + FR * GROUP)
        context = ctx[rows, :]
        turned = jnp.dot(context, order[...], preferred_element_type=F32).astype(BF16)
        for half in range(2):
            for part in range(2):
                at_lane = OH * half + PART * part
                lanes = slice(at_lane, at_lane + PART)
                weights = bufo[half, part].reshape(HD, PART)
                result = jnp.dot(
                    turned if half else context, weights, preferred_element_type=F32
                ) + mid[rows, lanes]
                for m, j in enumerate(group):
                    live = counts[0] > j
                    ostage[j, :, lanes] = jnp.where(
                        live, result[FR * m:FR * m + FR], 0.0
                    ).astype(BF16)
        book.start(None, lambda n=n: hand(n), ("h", n))

    by_role(book.close)
    book.close(None)
    for r in range(4):
        @pl.when(crossing[r])
        def _():
            book.close(("z", r))

        @pl.when(jnp.logical_not(crossing[r]))
        def _():
            book.close(("d", r))


def body(
    new_frames, conv_edges, kv_cache, norm_gains, conv_kernel,
    w_qkv, w_out, move_targets, lengths, counts,
):
    vmem = pl.BlockSpec(memory_space=pltpu.VMEM)
    smem = pl.BlockSpec(memory_space=pltpu.SMEM)
    any_ = pl.BlockSpec(memory_space=pl.ANY)
    dma = pltpu.SemaphoreType.DMA
    rows = SLOTS * FR
    out = pl.pallas_call(
        kernel,
        out_shape=jax.ShapeDtypeStruct((SLOTS, FR, D), BF16),
        in_specs=[any_, any_, any_, vmem, any_, any_, any_, smem, smem, smem],
        out_specs=any_,
        scratch_shapes=[
            pltpu.VMEM((SLOTS, FR, D), BF16),
            pltpu.VMEM((KERNEL, 1, D), F32),
            pltpu.VMEM((12, QW), BF16),
            pltpu.VMEM((6, D), BF16),
            pltpu.VMEM((SLOTS, EDGE, D), BF16),
            pltpu.VMEM((SLOTS, CTX, D), BF16),
            pltpu.VMEM((4, EDGE, D), BF16),
            pltpu.VMEM((4, CTX, D), BF16),
            pltpu.VMEM((4, EDGE, D), BF16),
            pltpu.VMEM((4, CTX, D), BF16),
            pltpu.VMEM((2, EDGE, D), BF16),
            pltpu.VMEM((2, CTX, D), BF16),
            pltpu.VMEM((12, WIDTHS[0]), BF16),
            pltpu.VMEM((12, WIDTHS[1]), BF16),
            pltpu.VMEM((6, OH), BF16),
            pltpu.VMEM((2, RING, RING, 24, WIDTHS[0] // 2), BF16),
            pltpu.VMEM((2, RING, RING, 24, WIDTHS[1] // 2), BF16),
            pltpu.VMEM((RING, 12, OH), BF16),
            pltpu.VMEM((2, 2, RING, 96, PART), BF16),
            pltpu.VMEM((24, WIDTHS[0] // 2), F32),
            pltpu.VMEM((96, OH), F32),
            pltpu.VMEM((48, D), F32),
            pltpu.VMEM((rows, D), F32),
            pltpu.VMEM((rows, D), BF16),
            pltpu.VMEM((rows, QW), BF16),
            pltpu.VMEM((rows, HD), BF16),
            pltpu.VMEM((160, 256), BF16),
            pltpu.VMEM((160, 256), F32),
            pltpu.VMEM((HD, HD), BF16),
            pltpu.VMEM((SLOTS, FR, D), BF16),
            dma((6,)), dma((2,)), dma((2,)), dma((8,)), dma((8,)),
            dma((16,)), dma((16,)), dma((8,)), dma((8,)),
            dma((16,)), dma((16,)), dma((16,)), dma((16,)),
            dma((18,)), dma((18,)), dma((18,)), dma((18,)),
            dma((4,)), dma((4,)), dma((4,)), dma((4,)),
        ],
        compiler_params=pltpu.CompilerParams(
            collective_id=0, has_side_effects=True, vmem_limit_bytes=56 * 2 ** 20
        ),
        cost_estimate=pl.CostEstimate(
            flops=2 * 10 ** 9, bytes_accessed=6 * 10 ** 6, transcendentals=10 ** 5
        ),
    )(
        new_frames[0], conv_edges[0], kv_cache[0], norm_gains[0], conv_kernel.transpose(1, 0, 2),
        w_qkv[0], w_out[0], move_targets, lengths, counts,
    )
    return out[None]


def solution(mesh):
    placed = (
        P("section", "sess", None, None),
        P("section", "sess", None, None),
        P("section", "sess", None, None),
        P("section", None, None),
        P("section", None, None),
        P("section", "sess", None),
        P("section", "sess", None),
        P("sess"),
        P("sess"),
        P("sess"),
    )
    return jax.shard_map(
        body,
        mesh=mesh,
        in_specs=placed,
        out_specs=P("section", "sess", None, None),
        check_vma=False,
    )
```
